256 devices in a mesh: prow: 32 (over y, x, core), pcol: 8 (over z).
Axes of the slice: x: 4, y: 4, z: 8, core: 2. Of those that a mesh axis runs over, the one named last changes fastest.
Arguments:
- right_side: bfloat16 [24576, 256], P('prow'), may hold values from -6 to 6
- l_factor: bfloat16 [24576, 24576], P('prow', 'pcol'), may hold values from -0.078125 to 0.078125
- u_factor: bfloat16 [24576, 24576], P('prow', 'pcol'), may hold values from -0.078125 to 0.078125
- l_pattern: int32 [192, 192], P('prow', 'pcol'), may hold values from 0 to 1, as said below
- u_pattern: int32 [192, 192], P('prow', 'pcol'), may hold values from 0 to 1, as said below
- l_inverse: bfloat16 [192, 128, 128], P('prow')
- u_inverse: bfloat16 [192, 128, 128], P('prow')
Outputs:
- forward: bfloat16 [24576, 256], P('prow')
- solution: bfloat16 [24576, 256], P('prow')
The draws below stay inside these ranges and needn't reach their ends.
Inputs may be any that keep to these rules, and one draw needn't show every extreme that they name: 0 or 1; with g = k // 6 and v = k mod 6 for supernode k, l_pattern[i, j] is 0 unless v_j < v_i and g_j >> v_i equals g_i >> v_i (j descends from i's separator). 0 or 1; u_pattern[i, j] is 0 unless v_j > v_i and g_i >> v_j equals g_j >> v_j (j lies on a separator above i).
All inputs are finite; a program needn't handle non-finite values.
Results may differ from the reference program's by a relative error of at most 0.015.
Values may be sent and summed in bfloat16 or wider, within the bound.
A program may use at most 128 MiB of HBM per device.

```python
import jax
import jax.numpy as jnp
from jax import lax

SB = 128
LEVELS = 6
NRHS = 256
NS = 192
N_ORDER = 24576


def pattern_draw(key, below):
    index = jnp.arange(NS, dtype=jnp.int32)
    levels = index % LEVELS
    groups = index // LEVELS
    row_level = levels[:, None]
    col_level = levels[None, :]
    row_group = groups[:, None]
    col_group = groups[None, :]
    if below:
        same_tree = jnp.right_shift(col_group, row_level) == jnp.right_shift(row_group, row_level)
        allowed = (col_level < row_level) & same_tree
    else:
        same_tree = jnp.right_shift(row_group, col_level) == jnp.right_shift(col_group, col_level)
        allowed = (col_level > row_level) & same_tree
    keep = jax.random.randint(key, (NS, NS), 0, 4) >= 1
    return jnp.where(allowed & keep, 1, 0).astype(jnp.int32)


def inverse_draw(key, spread):
    key_diag, key_off = jax.random.split(key)
    diag = jax.random.uniform(key_diag, (NS, SB, 1), jnp.float32, 0.6, 1.5)
    off = jax.random.normal(key_off, (NS, SB, SB), jnp.float32) * spread
    eye = jnp.eye(SB, dtype=jnp.float32)[None]
    return (eye * diag + off * SB ** (-0.5)).astype(jnp.bfloat16)


def draw_l_pattern(key, part):
    key = jax.random.fold_in(key, 11)
    return pattern_draw(key, True)


def draw_u_pattern(key, part):
    key = jax.random.fold_in(key, 12)
    return pattern_draw(key, False)


def draw_l_inverse(key, part):
    key = jax.random.fold_in(key, 13)
    return inverse_draw(key, 0.35)


def draw_u_inverse(key, part):
    key = jax.random.fold_in(key, 14)
    return inverse_draw(key, 0.35)


def block_scale(stream_key, dims, cuts, smallest, largest):
    level = 1.0
    for position, parts in cuts:
        draws = jax.random.uniform(jax.random.fold_in(jax.random.fold_in(stream_key, 6), position), (parts,), jnp.float32, smallest / len(cuts), largest / len(cuts))
        level = level * jnp.repeat(jnp.exp(draws), dims[position] // parts).reshape((-1,) + (1,) * (len(dims) - 1 - position))
    return level


def centred(key, dims, width, reach, cuts=(), kind=jnp.bfloat16):
    entries = width * jax.random.normal(key, dims, jnp.float32)
    if cuts:
        entries = entries * block_scale(key, dims, cuts, -0.22, 0.18)
    return jnp.clip(entries, -reach, reach).astype(kind)


def setup_inputs(seed: int = 0) -> dict:
    seeds = jax.random.split(jax.random.key(seed), 8)
    return {
        "right_side": centred(seeds[0], (N_ORDER, NRHS), 1.0, 6.0, ((0, 32),)),
        "l_factor": centred(seeds[1], (N_ORDER, N_ORDER), (SB * 48) ** -0.5, 0.078125, ((0, 32), (1, 8))),
        "u_factor": centred(seeds[2], (N_ORDER, N_ORDER), (SB * 48) ** -0.5, 0.078125, ((0, 32), (1, 8))),
        "l_pattern": draw_l_pattern(jax.random.fold_in(seeds[7], 71), 0),
        "u_pattern": draw_u_pattern(jax.random.fold_in(seeds[7], 71), 0),
        "l_inverse": draw_l_inverse(jax.random.fold_in(seeds[7], 71), 0),
        "u_inverse": draw_u_inverse(jax.random.fold_in(seeds[7], 71), 0),
    }


def sweep(factor, pattern, inverse, rhs, upward):
    groups = NS // LEVELS
    blocks = factor.reshape(groups, LEVELS, SB, groups, LEVELS, SB)
    mask = pattern.reshape(groups, LEVELS, groups, LEVELS)
    inverse4 = inverse.reshape(groups, LEVELS, SB, SB).astype(jnp.float32)
    rhs4 = rhs.reshape(groups, LEVELS, SB, NRHS)
    solved = [None] * LEVELS
    order = list(range(LEVELS)) if upward else list(range(LEVELS - 1, -1, -1))
    for level in order:
        if upward:
            low, high = 0, level
        else:
            low, high = level + 1, LEVELS
        if high > low:
            rows = blocks[:, level, :, :, low:high, :].astype(jnp.float32)
            rows = rows * mask[:, level, :, low:high][:, None, :, :, None].astype(jnp.float32)
            known = jnp.stack([solved[q] for q in range(low, high)], axis=1).astype(jnp.float32)
            partial_sum = jnp.einsum("tapqb,pqbn->tan", rows, known)
        else:
            partial_sum = jnp.zeros((groups, SB, NRHS), jnp.float32)
        resid = (rhs4[:, level].astype(jnp.float32) - partial_sum).astype(jnp.bfloat16)
        resid = lax.optimization_barrier(resid).astype(jnp.float32)
        solved[level] = jnp.einsum("tab,tbn->tan", inverse4[:, level], resid).astype(jnp.bfloat16)
    return jnp.stack(solved, axis=1).reshape(NS * SB, NRHS)


def reference(right_side, l_factor, u_factor, l_pattern, u_pattern, l_inverse, u_inverse):
    forward = sweep(l_factor, l_pattern, l_inverse, right_side, True)
    solution = sweep(u_factor, u_pattern, u_inverse, forward, False)
    return (forward, solution)
```

```python
import functools

import jax
import jax.numpy as jnp
from jax import lax
from jax.experimental import pallas as pl
from jax.experimental.pallas import tpu as pltpu
from jax.sharding import PartitionSpec as P

MESH = pl.DeviceIdType.MESH
BF = jnp.bfloat16
F32 = jnp.float32
TOP = (1, 5)

SEMS = (
    "rhs", "li", "ui",
    "l1", "l2", "l3", "l4", "l5", "u0", "u1", "u2", "u3", "u4",
    "s_rhs", "s_li", "s_ui", "s_l1", "s_l2", "s_lb", "s_ub", "s_ud",
    "y0", "y1", "y2", "f3", "f4", "f5",
    "t43", "t53", "t54", "t45", "t34", "t35",
    "ty3a", "ty3b", "ty4", "tx5", "tx4",
    "x5", "x4", "x3", "fb0", "fb1", "fb2", "cx2",
    "of", "os",
    "snd_all", "snd_diag", "snd_ntop", "snd_quad", "snd_quad_ntop", "snd_pair_ntop", "snd_top", "snd_ndiag", "snd_top_far", "snd_x4",
    "xl",
)
SEM = {name: i for i, name in enumerate(SEMS)}


def dot(a, b):
    return jnp.dot(a, b, preferred_element_type=F32)


def kernel(
    rhs, lf, uf, lp, up, li, ui, of, os,
    rb, lib, uib, ls, us, l1b, l2b, lb, ub, u12, u02, u01,
    mtl, mtu, lt43, lt53, lt54, ut45, ut34, ut35,
    yo, xo, yb, part, f3, f4, f5, yt3, yt4, xt5, xt4, xb5, xb4, xb3, acc, bpart, fb, xc2,
    sem,
):
    p = lax.axis_index("prow")
    z = lax.axis_index("pcol")
    q, k = p // 2, p % 2
    zd = q // 2
    half = q % 2
    top = 1 + 4 * k
    other_top = 5 - 4 * k
    diag = z == zd
    pair = z // 2 == q // 4
    quad = z // 4 == q // 8
    is_top = z == top
    not_top = z != top
    me = pl.multiple_of(k * 128, 128)

    def S(name):
        return sem.at[SEM[name]]

    def dev(qq, kk, zz):
        return (qq * 2 + kk, zz)

    sent = {}

    def send(src, dst, cond, rsem, device, units):
        pltpu.make_async_remote_copy(
            src_ref=src, dst_ref=dst, send_sem=S("snd_" + cond), recv_sem=S(rsem), device_id=device, device_id_type=MESH
        ).start()
        sent[cond] = sent.get(cond, 0) + units

    def local(src, dst, s):
        pltpu.make_async_copy(src, dst, S(s)).start()

    def wait(ref, s):
        pltpu.make_async_copy(ref, ref, S(s)).wait()

    def rows(ref, start, size, align=128):
        return ref.at[pl.ds(pl.multiple_of(start, align), size)]

    def when(c):
        return pl.when(c)

    sib = dev(q, 1 - k, z)

    bar = pltpu.get_barrier_semaphore()

    def hello(device):
        pl.semaphore_signal(bar, inc=1, device_id=device, device_id_type=MESH)

    for d in range(1, 16):
        hello(dev(q ^ d, k, z))
    for j in range(1, 8):
        hello(dev(q, k, (z + j) % 8))
    for j in range(8):
        hello(dev(q, 1 - k, (z + j) % 8))
    far = jnp.logical_and(is_top, zd != top)
    near = jnp.logical_and(not_top, pair)

    @when(far)
    def _():
        for d in range(1, 4):
            hello(dev(q ^ d, k, zd))

    @when(jnp.logical_and(near, diag))
    def _():
        hello(dev(q ^ 1, k, top))

    @when(jnp.logical_and(near, jnp.logical_not(diag)))
    def _():
        hello(dev(2 * z, k, top))
        hello(dev(2 * z + 1, k, top))

    local(rhs.at[:, pl.ds(me, 128)], rb.at[k], "rhs")
    local(li, lib.at[k], "li")
    for v in range(1, 6):
        local(lf.at[pl.ds(v * 128, 128), :], ls.at[pl.ds((v - 1) * 128, 128), :], "l%d" % v)
    local(ui, uib.at[k], "ui")
    for w in (4, 3, 0, 1, 2):
        local(uf.at[pl.ds(w * 128, 128), :], us.at[pl.ds(w * 128, 128), :], "u%d" % w)

    def mask(stage, pattern, srow, prow, col, dst, drow, dcol):
        block = stage[pl.ds(srow, 128), pl.ds(pl.multiple_of(col * 128, 128), 128)]
        keep = pattern[prow, col].astype(F32)
        dst[pl.ds(pl.multiple_of(drow, 128), 128), pl.ds(pl.multiple_of(dcol, 128), 128)] = (
            block.astype(F32) * keep
        ).astype(BF)

    def each_group(body):
        def step(j, carry):
            body(j)
            return carry

        lax.fori_loop(0, 4, step, 0)

    def each_own(body):
        for j2 in range(2):
            body(j2, 2 * half + j2)

    @when(diag)
    def _():
        wait(ls.at[pl.ds(0, 128), :], "l1")
        each_own(lambda j2, j: mask(ls, lp, 0, 1, j * 6, l1b, me, j2 * 128))
        wait(ls.at[pl.ds(128, 128), :], "l2")

        def level2(j):
            for w in range(2):
                mask(ls, lp, 128, 2, j * 6 + w, l2b, me, w * 512 + j * 128)

        each_group(level2)

    @when(jnp.logical_not(diag))
    def _():
        wait(ls.at[pl.ds(0, 128), :], "l1")
        wait(ls.at[pl.ds(128, 128), :], "l2")

    near_diag = jnp.logical_and(near, diag)
    near_rest = jnp.logical_and(near, jnp.logical_not(diag))
    for cond, count in ((far, 33), (near_diag, 31), (near_rest, 32)):
        @when(cond)
        def _(count=count):
            pl.semaphore_wait(bar, count)

    @when(jnp.logical_not(jnp.logical_or(far, near)))
    def _():
        pl.semaphore_wait(bar, 30)

    send(rhs.at[:, pl.ds(pl.multiple_of((1 - k) * 128, 128), 128)], rb.at[k], "all", "s_rhs", sib, 6)
    send(li, lib.at[k], "all", "s_li", sib, 6)

    @when(diag)
    def _():
        send(l1b.at[pl.ds(me, 128)], l1b.at[pl.ds(me, 128)], "diag", "s_l1", sib, 2)
        send(l2b.at[pl.ds(me, 128)], l2b.at[pl.ds(me, 128)], "diag", "s_l2", sib, 8)

    def to_top(src, dst, column, name, everywhere):
        view = dst.at[pl.ds(me, 128), pl.ds(pl.multiple_of(column * 512, 512), 512)]
        always, remote = ("all", "ntop") if everywhere else ("quad", "quad_ntop")

        def go():
            send(src, view, always, name, dev(q, 1 - k, other_top), 4)

            @when(is_top)
            def _():
                local(src, view, name)

            @when(not_top)
            def _():
                send(src, view, remote, name, dev(q, k, top), 4)

        if everywhere:
            go()
        else:
            when(quad)(go)

    for v in (3, 4, 5):
        srow = (v - 1) * 128
        wait(ls.at[pl.ds(srow, 128), :], "l%d" % v)

        def low(j, v=v, srow=srow):
            for w in range(3):
                mask(ls, lp, srow, v, j * 6 + w, lb, (v - 3) * 256 + me, w * 512 + j * 128)
            if v == 4:
                mask(ls, lp, srow, v, j * 6 + 3, mtl, 0, j * 128)
            if v == 5:
                mask(ls, lp, srow, v, j * 6 + 3, mtl, 128, j * 128)
                mask(ls, lp, srow, v, j * 6 + 4, mtl, 256, j * 128)

        each_group(low)
        mine = rows(lb, (v - 3) * 256 + me, 128)
        send(mine, mine, "all", "s_lb", sib, 12)
        if v == 4:
            to_top(mtl.at[pl.ds(0, 128)], lt43, z % 4, "t43", False)
        if v == 5:
            to_top(mtl.at[pl.ds(256, 128)], lt54, z, "t54", True)
            to_top(mtl.at[pl.ds(128, 128)], lt53, z, "t53", True)

    wait(rb.at[0], "rhs")
    wait(lib.at[0], "li")
    wait(rb.at[0], "s_rhs")
    wait(lib.at[0], "s_li")

    def solve(inverse, level, resid):
        for g in range(2):
            part = resid[g * 128 : (g + 1) * 128].astype(BF)
            yield dot(inverse[g, level], part).astype(BF)

    def right(level):
        return jnp.concatenate([rb[g, pl.ds(level * 128, 128), :] for g in range(2)], axis=0).astype(F32)

    def keep(store, level, resid, inverse):
        for g, value in enumerate(solve(inverse, level, resid)):
            store[pl.ds(level * 256 + g * 128, 128), :] = value

    def own(store, level):
        return store[pl.ds(level * 256, 256), :]

    def own_at(store, level):
        return store.at[pl.ds(level * 256, 256)]

    keep(yo, 0, right(0), lib)
    place = half * 256

    def spread(level, first, last):
        for d in range(first, last):
            send(own_at(yo, level), rows(yb, level * 512 + place, 256), "diag", "y%d" % level, dev(q ^ d, k, z), 2)

    @when(diag)
    def _():
        spread(0, 1, 4)
        yb[pl.ds(pl.multiple_of(place, 256), 256), :] = own(yo, 0)
        wait(l1b.at[pl.ds(0, 128)], "s_l1")
        keep(yo, 1, right(1) - dot(l1b[...], own(yo, 0)), lib)
        spread(1, 1, 4)
        yb[pl.ds(pl.multiple_of(512 + place, 256), 256), :] = own(yo, 1)
        wait(l2b.at[pl.ds(0, 128)], "s_l2")
        wait(yb.at[pl.ds(0, 256)], "y0")
        wait(yb.at[pl.ds(0, 256)], "y1")
        keep(yo, 2, right(2) - dot(l2b[...], yb[pl.ds(0, 1024), :]), lib)
        spread(2, 1, 4)
        yb[pl.ds(pl.multiple_of(1024 + place, 256), 256), :] = own(yo, 2)
        for first, last in ((4, 8), (8, 16)):
            for level in range(3):
                spread(level, first, last)

    wait(us.at[pl.ds(512, 128), :], "u4")
    each_group(lambda j: mask(us, up, 512, 4, j * 6 + 5, mtu, 0, j * 128))
    to_top(mtu.at[pl.ds(0, 128)], ut45, z, "t45", True)
    wait(us.at[pl.ds(384, 128), :], "u3")

    def upper3(j):
        mask(us, up, 384, 3, j * 6 + 4, mtu, 128, j * 128)
        mask(us, up, 384, 3, j * 6 + 5, mtu, 256, j * 128)

    each_group(upper3)
    to_top(mtu.at[pl.ds(128, 128)], ut34, z % 4, "t34", False)
    to_top(mtu.at[pl.ds(256, 128)], ut35, z, "t35", True)
    wait(uib.at[0], "ui")
    send(uib.at[k], uib.at[k], "all", "s_ui", sib, 6)
    for w in range(3):
        wait(us.at[pl.ds(w * 128, 128), :], "u%d" % w)

        def high(j, w=w):
            for v in (3, 4, 5):
                mask(us, up, w * 128, w, j * 6 + v, ub, w * 256 + me, (v - 3) * 512 + j * 128)

        each_group(high)
        mine = rows(ub, w * 256 + me, 128)
        send(mine, mine, "all", "s_ub", sib, 12)

    @when(diag)
    def _():
        def near_columns(j):
            mask(us, up, 128, 1, j * 6 + 2, u12, me, j * 128)
            mask(us, up, 0, 0, j * 6 + 2, u02, me, j * 128)

        each_group(near_columns)
        each_own(lambda j2, j: mask(us, up, 0, 0, j * 6 + 1, u01, me, j2 * 128))
        for ref, units in ((u12, 4), (u02, 4), (u01, 2)):
            send(ref.at[pl.ds(me, 128)], ref.at[pl.ds(me, 128)], "diag", "s_ud", sib, units)

    wait(lb.at[pl.ds(0, 384)], "s_lb")

    @when(diag)
    def _():
        wait(yb.at[pl.ds(0, 256)], "y2")

    @when(jnp.logical_not(diag))
    def _():
        for level in range(3):
            wait(yb.at[pl.ds(0, 512)], "y%d" % level)

    def fold(level, dst, slot, cond, name):
        here = pl.ds((level - 3) * 256, 256)
        part[here, :] = dot(lb[here, :], yb[...]).astype(BF)
        target = rows(dst, slot * 256, 256)

        @when(is_top)
        def _():
            dst[pl.ds(pl.multiple_of(slot * 256, 256), 256), :] = part[here, :]

        @when(not_top)
        def _():
            send(part.at[here], target, cond, name, dev(q, k, top), 2)

    @when(pair)
    def _():
        fold(3, f3, z % 2, "pair_ntop", "f3")

    @when(quad)
    def _():
        fold(4, f4, z % 4, "quad_ntop", "f4")

    fold(5, f5, z, "ntop", "f5")

    def publish(store, level, out, name, cond):
        for g in range(2):
            src = store.at[pl.ds(level * 256 + g * 128, 128)]
            dst = out.at[pl.ds(level * 128, 128), pl.ds(me, 128)]
            for j in range(8):
                @when(g == k)
                def _(j=j, src=src, dst=dst):
                    if j == 0:
                        local(src, dst, name)
                    else:
                        send_raw(src, dst, cond, name, dev(q, k, (z + j) % 8))

                @when(g != k)
                def _(j=j, src=src, dst=dst):
                    send_raw(src, dst, cond, name, dev(q, 1 - k, (z + j) % 8))
        sent[cond] = sent.get(cond, 0) + 15

    def send_raw(src, dst, cond, rsem, device):
        pltpu.make_async_remote_copy(
            src_ref=src, dst_ref=dst, send_sem=S("snd_" + cond), recv_sem=S(rsem), device_id=device, device_id_type=MESH
        ).start()

    out0 = of.at[pl.ds(0, 128), pl.ds(me, 128)]
    local(rows(yo, me, 128), out0, "of")
    send(rows(yo, pl.multiple_of((1 - k) * 128, 128), 128), out0, "all", "of", sib, 1)

    @when(diag)
    def _():
        publish(yo, 1, of, "of", "diag")
        publish(yo, 2, of, "of", "diag")

    wait(uib.at[0], "s_ui")

    def total(ref, count):
        acc_value = ref[pl.ds(0, 256), :].astype(F32)
        for i in range(1, count):
            acc_value += ref[pl.ds(i * 256, 256), :].astype(F32)
        return acc_value

    @when(is_top)
    def _():
        @when(pair)
        def _():
            wait(f3.at[pl.ds(0, 256)], "f3")

        @when(jnp.logical_not(pair))
        def _():
            wait(f3, "f3")

        mine = pl.ds(pl.multiple_of(q * 256, 256), 256)
        mine_at = rows(yt3, q * 256, 256, 256)
        keep(yo, 3, right(3) - total(f3, 2), lib)
        for d in range(1, 8):
            send(own_at(yo, 3), mine_at, "top", "ty3a", dev(q ^ d, k, z), 2)
        for d in range(8, 16):
            send(own_at(yo, 3), mine_at, "top", "ty3b", dev(q ^ d, k, z), 2)
        yt3[mine, :] = own(yo, 3)

        @when(quad)
        def _():
            wait(f4.at[pl.ds(0, 768)], "f4")

        @when(jnp.logical_not(quad))
        def _():
            wait(f4, "f4")

        s4 = right(4) - total(f4, 4)
        wait(lt43, "t43")
        wait(yt3.at[pl.ds(0, 7 * 256)], "ty3a")
        eight = pl.ds(pl.multiple_of((q // 8) * 2048, 2048), 2048)
        keep(yo, 4, s4 - dot(lt43[...], yt3[eight, :]), lib)
        for d in range(1, 16):
            send(own_at(yo, 4), rows(yt4, q * 256, 256, 256), "top", "ty4", dev(q ^ d, k, z), 2)
        yt4[mine, :] = own(yo, 4)
        wait(yt3.at[pl.ds(0, 8 * 256)], "ty3b")
        wait(lt53, "t53")
        s5 = right(5) - dot(lt53[...], yt3[...])
        wait(f5.at[pl.ds(0, 7 * 256)], "f5")
        acc[...] = s5 - total(f5, 8)
        wait(lt54, "t54")
        wait(yt4.at[pl.ds(0, 15 * 256)], "ty4")
        keep(yo, 5, acc[...] - dot(lt54[...], yt4[...]), lib)
        keep(xo, 5, own(yo, 5).astype(F32), uib)
        for d in range(1, 16):
            send(own_at(xo, 5), rows(xt5, q * 256, 256, 256), "top", "tx5", dev(q ^ d, k, z), 2)
        xt5[mine, :] = own(xo, 5)
        wait(ut45, "t45")
        wait(xt5.at[pl.ds(0, 15 * 256)], "tx5")
        keep(xo, 4, own(yo, 4).astype(F32) - dot(ut45[...], xt5[...]), uib)
        in_eight = rows(xt4, (q % 8) * 256, 256, 256)
        for d in range(1, 8):
            send(own_at(xo, 4), in_eight, "top", "tx4", dev(q ^ d, k, z), 2)
        xt4[pl.ds(pl.multiple_of((q % 8) * 256, 256), 256), :] = own(xo, 4)
        for j in range(1, 8):
            zz = (z + j) % 8
            send(rows(xt5, zz * 512, 512, 512), xb5, "top", "x5", dev(q, k, zz), 4)
        xb5[...] = xt5[pl.ds(pl.multiple_of(z * 512, 512), 512), :]
        wait(ut35, "t35")
        acc[...] = own(yo, 3).astype(F32) - dot(ut35[...], xt5[...])
        wait(ut34, "t34")
        wait(xt4.at[pl.ds(0, 7 * 256)], "tx4")
        keep(xo, 3, acc[...] - dot(ut34[...], xt4[...]), uib)
        for d in range(1, 4):
            at = rows(xb3, half * 256, 256, 256)

            @when(zd == top)
            def _(d=d, at=at):
                send_raw(own_at(xo, 3), at, "top", "x3", dev(q ^ d, k, z))

            @when(zd != top)
            def _(d=d, at=at):
                send_raw(own_at(xo, 3), at, "top", "x3", dev(q ^ d, k, zd))

        sent["top"] += 6

        @when(zd == top)
        def _():
            xb3[pl.ds(pl.multiple_of(half * 256, 256), 256), :] = own(xo, 3)

        @when(zd != top)
        def _():
            send(own_at(xo, 3), rows(xb3, half * 256, 256, 256), "top_far", "x3", dev(q, k, zd), 2)

        for j in range(4):
            zz = (q // 8) * 4 + j
            src = rows(xt4, j * 512, 512, 512)

            @when(zz == z)
            def _(src=src):
                local(src, xb4, "xl")
                wait(xb4, "xl")

            @when(zz != z)
            def _(src=src, zz=zz):
                send_raw(src, xb4, "x4", "x4", dev(q, k, zz))

        for level in (3, 4, 5):
            publish(yo, level, of, "of", "top")
        for level in (5, 4, 3):
            publish(xo, level, os, "os", "top")

    wait(ub.at[pl.ds(0, 384)], "s_ub")

    @when(not_top)
    def _():
        wait(xb5, "x5")

    bpart[...] = dot(ub[:, pl.ds(1024, 512)], xb5[...])

    @when(quad)
    def _():
        @when(not_top)
        def _():
            wait(xb4, "x4")

        bpart[...] += dot(ub[:, pl.ds(512, 512)], xb4[...])

    @when(pair)
    def _():
        mine_too = jnp.logical_and(is_top, diag)

        @when(mine_too)
        def _():
            wait(xb3.at[pl.ds(0, 256)], "x3")

        @when(jnp.logical_not(mine_too))
        def _():
            wait(xb3, "x3")

        bpart[...] += dot(ub[:, pl.ds(0, 512)], xb3[...])

    @when(jnp.logical_not(diag))
    def _():
        for w in (2, 1, 0):
            here = pl.ds(w * 256, 256)
            part2 = bpart[here, :].astype(BF)
            xsend = fb.at[w, pl.ds(pl.multiple_of(z * 256, 256), 256)]
            fb[w, pl.ds(pl.multiple_of(z * 256, 256), 256), :] = part2
            send(xsend, xsend, "ndiag", "fb%d" % w, dev(q, k, zd), 2)

    @when(diag)
    def _():
        fb[:, pl.ds(pl.multiple_of(z * 256, 256), 256), :] = jnp.zeros((3, 256, 128), BF)

        def rest(w):
            wait(fb.at[w, pl.ds(0, 7 * 256)], "fb%d" % w)
            value = own(yo, w).astype(F32) - bpart[pl.ds(w * 256, 256), :]
            for i in range(8):
                value -= fb[w, pl.ds(i * 256, 256), :].astype(F32)
            return value

        keep(xo, 2, rest(2), uib)
        send(own_at(xo, 2), rows(xc2, place, 256, 256), "diag", "cx2", dev(q ^ 1, k, z), 2)
        xc2[pl.ds(pl.multiple_of(place, 256), 256), :] = own(xo, 2)
        publish(xo, 2, os, "os", "diag")
        r1 = rest(1)
        acc[...] = rest(0)
        wait(yt4.at[pl.ds(0, 1280)], "s_ud")
        wait(xc2.at[pl.ds(0, 256)], "cx2")
        keep(xo, 1, r1 - dot(u12[...], xc2[...]), uib)
        publish(xo, 1, os, "os", "diag")
        keep(xo, 0, acc[...] - dot(u02[...], xc2[...]) - dot(u01[...], own(xo, 1)), uib)
        publish(xo, 0, os, "os", "diag")

    wait(of, "of")
    wait(os, "os")
    where = {
        "all": None, "diag": diag, "ntop": not_top, "quad": quad, "quad_ntop": jnp.logical_and(quad, not_top),
        "pair_ntop": jnp.logical_and(pair, not_top), "top": is_top, "ndiag": jnp.logical_not(diag), "top_far": far,
    }
    @when(jnp.logical_and(is_top, quad))
    def _():
        wait(yt4.at[pl.ds(0, 12 * 128)], "snd_x4")

    @when(jnp.logical_and(is_top, jnp.logical_not(quad)))
    def _():
        wait(yt4.at[pl.ds(0, 16 * 128)], "snd_x4")

    for cond, units in sent.items():
        def drain(cond=cond, units=units):
            while units > 0:
                now = min(units, 32)
                wait(yt4.at[pl.ds(0, now * 128)], "snd_" + cond)
                units -= now

        if where[cond] is None:
            drain()
        else:
            when(where[cond])(drain)


def on_device(right_side, l_factor, u_factor, l_pattern, u_pattern, l_inverse, u_inverse):
    vm = lambda *shape: pltpu.VMEM(shape, BF)
    anywhere = pl.BlockSpec(memory_space=pl.ANY)
    smem = pl.BlockSpec(memory_space=pltpu.SMEM)
    scratch = [
        vm(2, 768, 128), vm(2, 6, 128, 128), vm(2, 6, 128, 128),
        vm(640, 3072), vm(640, 3072),
        vm(256, 256), vm(256, 1024), vm(768, 1536), vm(768, 1536), vm(256, 512), vm(256, 512), vm(256, 256),
        vm(384, 512), vm(384, 512),
        vm(256, 2048), vm(256, 4096), vm(256, 4096), vm(256, 4096), vm(256, 2048), vm(256, 4096),
        vm(1536, 128), vm(1536, 128), vm(1536, 128), vm(768, 128),
        vm(512, 128), vm(1024, 128), vm(2048, 128),
        vm(4096, 128), vm(4096, 128), vm(4096, 128), vm(2048, 128),
        vm(512, 128), vm(512, 128), vm(512, 128),
        pltpu.VMEM((256, 128), F32), pltpu.VMEM((768, 128), F32),
        vm(3, 2048, 128), vm(512, 128),
        pltpu.SemaphoreType.DMA((len(SEMS),)),
    ]
    return pl.pallas_call(
        kernel,
        out_shape=(jax.ShapeDtypeStruct((768, 256), BF), jax.ShapeDtypeStruct((768, 256), BF)),
        in_specs=[anywhere, anywhere, anywhere, smem, smem, anywhere, anywhere],
        out_specs=(anywhere, anywhere),
        scratch_shapes=scratch,
        compiler_params=pltpu.CompilerParams(collective_id=0, has_side_effects=True, vmem_limit_bytes=48 * 2**20),
        name="sweeps",
    )(right_side, l_factor, u_factor, l_pattern, u_pattern, l_inverse, u_inverse)


def solution(mesh):
    placed = (
        P("prow", None),
        P("prow", "pcol"),
        P("prow", "pcol"),
        P("prow", "pcol"),
        P("prow", "pcol"),
        P("prow", None, None),
        P("prow", None, None),
    )
    return jax.shard_map(
        on_device,
        mesh=mesh,
        in_specs=placed,
        out_specs=(P("prow", None), P("prow", None)),
        check_vma=False,
    )
```

```python
import jax
import jax.numpy as jnp
from jax import lax
from jax.experimental import pallas as pl
from jax.experimental.pallas import tpu as pltpu
from jax.sharding import PartitionSpec as P

MESH = pl.DeviceIdType.MESH
BF = jnp.bfloat16
F32 = jnp.float32
VMEM_LIMIT = 62 * 2**20

SEMS = (
    "rhs", "li", "ui", "lp", "up",
    "l1", "l2", "l3", "l4", "l5", "u0", "u1", "u2", "u3", "u4",
    "s_rhs", "s_li", "s_ui", "s_l1", "s_l2", "s_lb", "s_ub", "s_ud",
    "y0", "y1", "y2", "sc", "ag", "y3", "f3", "f4", "f5",
    "t43", "t54", "t45", "t34", "t35",
    "ty3a", "ty3b", "ty4", "tx5", "tx4",
    "x5", "x4", "x3", "tr1", "tr2", "fb0", "fb1", "fb2", "cx2",
    "of", "os", "xl",
)
CONDS = (
    "all", "diag", "ntop", "quad", "quad_ntop", "quad_top", "pair_ntop", "top", "top_far", "x4", "pair", "npair", "npair2",
    "odd", "two", "exit", "near",
)
SEM = {name: i for i, name in enumerate(SEMS + tuple("snd_" + c for c in CONDS))}


def dot(a, b):
    return jnp.dot(a, b, preferred_element_type=F32)


def kernel(
    rhs, lf, uf, lph, uph, li, ui, of, os,
    lp, up, rb, lib, uib, ls, us, l1b, l2b, lb, ub, u12, u02, u01,
    mtl, mtu, lt43, lt54, ut45, ut34, ut35,
    yo, xo, yb, part, f3, f4, f5, yt3, yt4, xt5, xt4, xb5, xb4, xb3, yb3, acc, bpart, bpb, fb, tb, xc2,
    sem,
):
    p = lax.axis_index("prow")
    z = lax.axis_index("pcol")
    q, k = p // 2, p % 2
    zd = q // 2
    half = q % 2
    top = 1 + 4 * k
    other_top = 5 - 4 * k
    block_row = z // 2
    diag = z == zd
    pair = block_row == q // 4
    quad = z // 4 == q // 8
    is_top = z == top
    not_top = z != top
    not_diag = z != zd
    not_pair = block_row != q // 4
    not_quad = z // 4 != q // 8
    me = pl.multiple_of(k * 128, 128)
    both = jnp.logical_and

    def S(name):
        return sem.at[SEM[name]]

    def dev(qq, kk, zz):
        return (qq * 2 + kk, zz)

    sent = {}

    def send_raw(src, dst, cond, rsem, device):
        pltpu.make_async_remote_copy(
            src_ref=src, dst_ref=dst, send_sem=S("snd_" + cond), recv_sem=S(rsem), device_id=device, device_id_type=MESH
        ).start()

    def send(src, dst, cond, rsem, device, units):
        send_raw(src, dst, cond, rsem, device)
        sent[cond] = sent.get(cond, 0) + units

    def local(src, dst, s):
        pltpu.make_async_copy(src, dst, S(s)).start()

    def wait(ref, s):
        pltpu.make_async_copy(ref, ref, S(s)).wait()

    def rows(ref, start, size, align=128):
        return ref.at[pl.ds(pl.multiple_of(start, align), size)]

    when = pl.when
    sib = dev(q, 1 - k, z)

    bar = pltpu.get_barrier_semaphore()

    def hello(device):
        pl.semaphore_signal(bar, inc=1, device_id=device, device_id_type=MESH)

    for d in range(1, 16):
        hello(dev(q ^ d, k, z))
    for j in range(1, 8):
        hello(dev(q, k, (z + j) % 8))
    for j in range(8):
        hello(dev(q, 1 - k, (z + j) % 8))
    far = both(is_top, zd != top)
    near = both(not_top, pair)
    near_diag = both(near, diag)
    near_rest = both(near, not_diag)

    @when(far)
    def _():
        for d in range(1, 4):
            hello(dev(q ^ d, k, zd))

    @when(near_diag)
    def _():
        hello(dev(q ^ 1, k, top))

    @when(near_rest)
    def _():
        hello(dev(2 * z, k, top))
        hello(dev(2 * z + 1, k, top))

    local(rhs.at[:, pl.ds(me, 128)], rb.at[k], "rhs")
    local(li, lib.at[k], "li")
    local(lph, lp, "lp")
    local(uph, up, "up")

    @when(diag)
    def _():
        for v in (1, 2):
            local(lf.at[pl.ds(v * 128, 128), :], ls.at[pl.ds((v - 1) * 128, 128), :], "l%d" % v)

    for v in (3, 4, 5):
        local(lf.at[pl.ds(v * 128, 128), :], ls.at[pl.ds((v - 1) * 128, 128), :], "l%d" % v)
    local(ui, uib.at[k], "ui")
    for w in (4, 3, 0, 1, 2):
        local(uf.at[pl.ds(w * 128, 128), :], us.at[pl.ds(w * 128, 128), :], "u%d" % w)

    def mask(stage, pattern, srow, prow, col, dst, drow, dcol):
        block = stage[pl.ds(srow, 128), pl.ds(pl.multiple_of(col * 128, 128), 128)]
        keep = jnp.full((128, 128), pattern[prow, col].astype(F32)).astype(BF)
        dst[pl.ds(pl.multiple_of(drow, 128), 128), pl.ds(pl.multiple_of(dcol, 128), 128)] = block * keep

    def each_group(body):
        def step(j, carry):
            body(j)
            return carry

        lax.fori_loop(0, 4, step, 0)

    def each_own(body):
        for j2 in range(2):
            body(j2, 2 * half + j2)

    pltpu.make_async_copy(lph, lp, S("lp")).wait()
    pltpu.make_async_copy(uph, up, S("up")).wait()

    @when(diag)
    def _():
        wait(ls.at[pl.ds(0, 128), :], "l1")
        each_own(lambda j2, j: mask(ls, lp, 0, 1, j * 6, l1b, me, j2 * 128))
        wait(ls.at[pl.ds(128, 128), :], "l2")

        def level2(j):
            for w in range(2):
                mask(ls, lp, 128, 2, j * 6 + w, l2b, me, w * 512 + j * 128)

        each_group(level2)

    for cond, count in ((far, 33), (near_diag, 31), (near_rest, 32)):
        @when(cond)
        def _(count=count):
            pl.semaphore_wait(bar, count)

    @when(jnp.logical_not(jnp.logical_or(far, near)))
    def _():
        pl.semaphore_wait(bar, 30)

    send(rhs.at[:, pl.ds(pl.multiple_of((1 - k) * 128, 128), 128)], rb.at[k], "all", "s_rhs", sib, 6)
    send(li, lib.at[k], "all", "s_li", sib, 6)

    @when(diag)
    def _():
        send(l1b.at[pl.ds(me, 128)], l1b.at[pl.ds(me, 128)], "diag", "s_l1", sib, 2)
        send(l2b.at[pl.ds(me, 128)], l2b.at[pl.ds(me, 128)], "diag", "s_l2", sib, 8)

    def to_top(src, dst, column, name, everywhere, who):
        view = dst.at[pl.ds(me, 128), pl.ds(pl.multiple_of(column * 512, 512), 512)]

        def from_rest():
            cond = "ntop" if everywhere else "quad_ntop"
            send(src, view, cond, name, dev(q, k, top), 4)
            send(src, view, cond, name, dev(q, 1 - k, other_top), 4)

        def from_top():
            local(src, view, name)
            send(src, view, "top" if everywhere else "quad_top", name, dev(q, 1 - k, other_top), 4)

        for mine, go in ((not_top, from_rest), (is_top, from_top)):
            if who is None or who == (mine is is_top):
                when(mine if everywhere else both(mine, quad))(go)

    def solve(inverse, level, resid):
        for g in range(2):
            piece = resid[g * 128 : (g + 1) * 128].astype(BF)
            yield dot(inverse[g, level], piece).astype(BF)

    def right(level):
        return jnp.concatenate([rb[g, pl.ds(level * 128, 128), :] for g in range(2)], axis=0).astype(F32)

    def keep(store, level, resid, inverse):
        for g, value in enumerate(solve(inverse, level, resid)):
            store[pl.ds(level * 256 + g * 128, 128), :] = value

    def own(store, level):
        return store[pl.ds(level * 256, 256), :]

    def own_at(store, level):
        return store.at[pl.ds(level * 256, 256)]

    def put(ref, start, size, value):
        ref[pl.ds(pl.multiple_of(start, size), size), :] = value

    wait(rb.at[0], "rhs")
    wait(lib.at[0], "li")
    wait(rb.at[0], "s_rhs")
    wait(lib.at[0], "s_li")
    keep(yo, 0, right(0), lib)
    place = half * 256

    def spread(level):
        for d in range(1, 4):
            send(own_at(yo, level), rows(yb, level * 512 + place, 256), "diag", "y%d" % level, dev(q ^ d, k, z), 2)

    @when(diag)
    def _():
        spread(0)
        wait(l1b.at[pl.ds(0, 128)], "s_l1")
        keep(yo, 1, right(1) - dot(l1b[...], own(yo, 0)), lib)
        spread(1)
        put(yb, place, 256, own(yo, 0))
        put(yb, 512 + place, 256, own(yo, 1))

    for v in (3, 4, 5):
        srow = (v - 1) * 128
        wait(ls.at[pl.ds(srow, 128), :], "l%d" % v)

        def low(j, v=v, srow=srow):
            for w in range(3 if v < 5 else 4):
                mask(ls, lp, srow, v, j * 6 + w, lb, (v - 3) * 256 + me, w * 512 + j * 128)
            if v == 4:
                mask(ls, lp, srow, v, j * 6 + 3, mtl, 0, j * 128)
            if v == 5:
                mask(ls, lp, srow, v, j * 6 + 4, mtl, 128, j * 128)

        each_group(low)
        width = 1536 if v < 5 else 2048
        mine = lb.at[pl.ds(pl.multiple_of((v - 3) * 256 + me, 128), 128), pl.ds(0, width)]
        send(mine, mine, "all", "s_lb", sib, width // 128)
        if v == 4:
            to_top(mtl.at[pl.ds(0, 128)], lt43, z % 4, "t43", False, None)
        if v == 5:
            to_top(mtl.at[pl.ds(128, 128)], lt54, z, "t54", True, None)

    @when(diag)
    def _():
        wait(l2b.at[pl.ds(0, 128)], "s_l2")
        wait(yb.at[pl.ds(0, 256)], "y0")
        wait(yb.at[pl.ds(0, 256)], "y1")
        keep(yo, 2, right(2) - dot(l2b[...], yb[pl.ds(0, 1024), :]), lib)
        spread(2)
        put(yb, 1024 + place, 256, own(yo, 2))

    wait(us.at[pl.ds(512, 128), :], "u4")
    each_group(lambda j: mask(us, up, 512, 4, j * 6 + 5, mtu, 0, j * 128))
    wait(us.at[pl.ds(384, 128), :], "u3")

    def upper3(j):
        mask(us, up, 384, 3, j * 6 + 4, mtu, 128, j * 128)
        mask(us, up, 384, 3, j * 6 + 5, mtu, 256, j * 128)

    each_group(upper3)
    wait(uib.at[0], "ui")

    def fold_at(level):
        return pl.ds((level - 3) * 256, 256)

    def fold_here(level, dst, slot):
        put(dst, slot * 256, 256, part[fold_at(level), :])

    def fold_there(level, dst, slot, cond, name):
        send(part.at[fold_at(level)], rows(dst, slot * 256, 256), cond, name, dev(q, k, top), 2)

    def low_part(level):
        return dot(lb[fold_at(level), pl.ds(0, 1536)], yb[...])

    wait(lb.at[pl.ds(0, 320)], "s_lb")

    @when(diag)
    def _():
        wait(yb.at[pl.ds(0, 256)], "y2")

    @when(both(pair, not_diag))
    def _():
        for level in range(3):
            wait(yb.at[pl.ds(0, 512)], "y%d" % level)

    def piece(owner):
        return rows(yb, owner * 96, 96, 32)

    @when(pair)
    def _():
        part[fold_at(3), :] = low_part(3).astype(BF)

        @when(is_top)
        def _():
            fold_here(3, f3, z % 2)

        @when(not_top)
        def _():
            fold_there(3, f3, z % 2, "pair_ntop", "f3")

        for d in (4, 8, 12):
            send(piece(q ^ d), piece(q ^ d), "pair", "sc", dev(q ^ d, k, z), 3 / 4)
        for d in range(4, 16):
            send(piece(q), piece(q), "pair", "ag", dev(q ^ d, k, z), 3 / 4)

    @when(not_pair)
    def _():
        wait(yb.at[pl.ds(0, 96)], "sc")
        for d in range(1, 4):
            send(piece(q), piece(q), "npair", "ag", dev(q ^ d, k, z), 3 / 4)
        for e in range(1, 4):
            @when((q // 4) ^ e != block_row)
            def _(e=e):
                for d in range(4 * e, 4 * e + 4):
                    send_raw(piece(q), piece(q), "npair2", "ag", dev(q ^ d, k, z))
        wait(yb.at[pl.ds(0, 15 * 96)], "ag")

    sent["npair2"] = 6

    @when(quad)
    def _():
        part[fold_at(4), :] = low_part(4).astype(BF)

        @when(is_top)
        def _():
            fold_here(4, f4, z % 4)

        @when(not_top)
        def _():
            fold_there(4, f4, z % 4, "quad_ntop", "f4")

    to_top(mtu.at[pl.ds(0, 128)], ut45, z, "t45", True, None)
    send(uib.at[k], uib.at[k], "all", "s_ui", sib, 6)
    for w in range(3):
        wait(us.at[pl.ds(w * 128, 128), :], "u%d" % w)

        def high(j, w=w):
            for v in (3, 4, 5):
                mask(us, up, w * 128, w, j * 6 + v, ub, w * 256 + me, (v - 3) * 512 + j * 128)

        each_group(high)
        mine = rows(ub, w * 256 + me, 128)
        send(mine, mine, "all", "s_ub", sib, 12)

    @when(diag)
    def _():
        def near_columns(j):
            mask(us, up, 128, 1, j * 6 + 2, u12, me, j * 128)
            mask(us, up, 0, 0, j * 6 + 2, u02, me, j * 128)

        each_group(near_columns)
        each_own(lambda j2, j: mask(us, up, 0, 0, j * 6 + 1, u01, me, j2 * 128))
        for ref, units in ((u12, 4), (u02, 4), (u01, 2)):
            send(ref.at[pl.ds(me, 128)], ref.at[pl.ds(me, 128)], "diag", "s_ud", sib, units)

    def sum5():
        mixed = acc[...] + dot(lb[fold_at(5), pl.ds(1536, 512)], yb3[...])
        part[fold_at(5), :] = mixed.astype(BF)

    def upper_to_top(who):
        to_top(mtu.at[pl.ds(128, 128)], ut34, z % 4, "t34", False, who)
        to_top(mtu.at[pl.ds(256, 128)], ut35, z, "t35", True, who)

    def publish(store, level, out, name, cond):
        dst = out.at[pl.ds(level * 128, 128), pl.ds(me, 128)]
        for flip in (0, 1):
            core = (k + flip) % 2
            src = rows(store, level * 256 + core * 128, 128)
            for j in range(8):
                if flip == 0 and j == 0:
                    local(src, dst, name)
                else:
                    send(src, dst, cond, name, dev(q, core, (z + j) % 8), 1)

    out0 = of.at[pl.ds(0, 128), pl.ds(me, 128)]
    local(rows(yo, me, 128), out0, "of")
    send(rows(yo, pl.multiple_of((1 - k) * 128, 128), 128), out0, "all", "of", sib, 1)
    acc[...] = low_part(5)
    wait(uib.at[0], "s_ui")

    @when(not_top)
    def _():
        wait(yb3, "y3")
        sum5()
        fold_there(5, f5, z, "ntop", "f5")
        upper_to_top(False)

    @when(diag)
    def _():
        publish(yo, 1, of, "of", "diag")
        publish(yo, 2, of, "of", "diag")

    def total(ref, count):
        value = ref[pl.ds(0, 256), :].astype(F32)
        for i in range(1, count):
            value += ref[pl.ds(i * 256, 256), :].astype(F32)
        return value

    @when(is_top)
    def _():
        @when(pair)
        def _():
            wait(f3.at[pl.ds(0, 256)], "f3")

        @when(not_pair)
        def _():
            wait(f3, "f3")

        keep(yo, 3, right(3) - total(f3, 2), lib)
        for d in range(1, 8):
            send(own_at(yo, 3), rows(yt3, q * 256, 256, 256), "top", "ty3a", dev(q ^ d, k, z), 2)
        for d in range(8, 16):
            send(own_at(yo, 3), rows(yt3, q * 256, 256, 256), "top", "ty3b", dev(q ^ d, k, z), 2)
        put(yt3, q * 256, 256, own(yo, 3))
        wait(yt3.at[pl.ds(0, 7 * 256)], "ty3a")
        wait(yt3.at[pl.ds(0, 8 * 256)], "ty3b")
        for j in range(1, 8):
            zz = (z + j) % 8
            send(rows(yt3, zz * 512, 512, 512), yb3, "top", "y3", dev(q, k, zz), 4)
        yb3[...] = yt3[pl.ds(pl.multiple_of(z * 512, 512), 512), :]

        @when(quad)
        def _():
            wait(f4.at[pl.ds(0, 768)], "f4")

        @when(not_quad)
        def _():
            wait(f4, "f4")

        s4 = right(4) - total(f4, 4)
        wait(lt43, "t43")
        eight = pl.ds(pl.multiple_of((q // 8) * 2048, 2048), 2048)
        keep(yo, 4, s4 - dot(lt43[...], yt3[eight, :]), lib)
        for d in range(1, 16):
            send(own_at(yo, 4), rows(yt4, q * 256, 256, 256), "top", "ty4", dev(q ^ d, k, z), 2)
        put(yt4, q * 256, 256, own(yo, 4))
        sum5()
        fold_here(5, f5, z)
        upper_to_top(True)
        publish(yo, 3, of, "of", "top")
        wait(f5.at[pl.ds(0, 7 * 256)], "f5")
        acc[...] = right(5) - total(f5, 8)
        wait(lt54, "t54")
        wait(yt4.at[pl.ds(0, 15 * 256)], "ty4")
        keep(yo, 5, acc[...] - dot(lt54[...], yt4[...]), lib)
        keep(xo, 5, own(yo, 5).astype(F32), uib)
        for d in range(1, 16):
            send(own_at(xo, 5), rows(xt5, q * 256, 256, 256), "top", "tx5", dev(q ^ d, k, z), 2)
        put(xt5, q * 256, 256, own(xo, 5))
        publish(yo, 4, of, "of", "top")
        wait(ut45, "t45")
        wait(xt5.at[pl.ds(0, 15 * 256)], "tx5")
        keep(xo, 4, own(yo, 4).astype(F32) - dot(ut45[...], xt5[...]), uib)
        for d in range(1, 8):
            send(own_at(xo, 4), rows(xt4, (q % 8) * 256, 256, 256), "top", "tx4", dev(q ^ d, k, z), 2)
        put(xt4, (q % 8) * 256, 256, own(xo, 4))
        for j in range(1, 8):
            zz = (z + j) % 8
            send(rows(xt5, zz * 512, 512, 512), xb5, "top", "x5", dev(q, k, zz), 4)
        xb5[...] = xt5[pl.ds(pl.multiple_of(z * 512, 512), 512), :]
        publish(yo, 5, of, "of", "top")
        wait(ut35, "t35")
        acc[...] = own(yo, 3).astype(F32) - dot(ut35[...], xt5[...])
        wait(ut34, "t34")
        wait(xt4.at[pl.ds(0, 7 * 256)], "tx4")
        keep(xo, 3, acc[...] - dot(ut34[...], xt4[...]), uib)
        at = rows(xb3, half * 256, 256, 256)
        for d in range(1, 4):
            @when(zd == top)
            def _(d=d):
                send_raw(own_at(xo, 3), at, "top", "x3", dev(q ^ d, k, z))

            @when(zd != top)
            def _(d=d):
                send_raw(own_at(xo, 3), at, "top", "x3", dev(q ^ d, k, zd))

        sent["top"] += 6

        @when(zd == top)
        def _():
            put(xb3, half * 256, 256, own(xo, 3))

        @when(zd != top)
        def _():
            send(own_at(xo, 3), at, "top_far", "x3", dev(q, k, zd), 2)

        for j in range(4):
            zz = (q // 8) * 4 + j
            src = rows(xt4, j * 512, 512, 512)

            @when(zz == z)
            def _(src=src):
                local(src, xb4, "xl")
                wait(xb4, "xl")

            @when(zz != z)
            def _(src=src, zz=zz):
                send_raw(src, xb4, "x4", "x4", dev(q, k, zz))

        for level in (5, 4, 3):
            publish(xo, level, os, "os", "top")

    wait(ub.at[pl.ds(0, 384)], "s_ub")

    @when(not_top)
    def _():
        wait(xb5, "x5")

    bpart[...] = dot(ub[:, pl.ds(1024, 512)], xb5[...])

    @when(quad)
    def _():
        @when(not_top)
        def _():
            wait(xb4, "x4")

        bpart[...] += dot(ub[:, pl.ds(512, 512)], xb4[...])

    @when(pair)
    def _():
        mine_too = both(is_top, diag)

        @when(mine_too)
        def _():
            wait(xb3.at[pl.ds(0, 256)], "x3")

        @when(jnp.logical_not(mine_too))
        def _():
            wait(xb3, "x3")

        bpart[...] += dot(ub[:, pl.ds(0, 512)], xb3[...])

    def to_diag(slot, cond):
        for w in (2, 1, 0):
            here = pl.ds(w * 256, 256)
            bpb[here, :] = bpart[here, :].astype(BF)
            send(bpb.at[here], fb.at[w, pl.ds(pl.multiple_of(slot * 256, 256), 256)], cond, "fb%d" % w, dev(q, k, zd), 2)

    @when(both(quad, not_diag))
    def _():
        to_diag(jnp.where(pair, 0, 1 + z % 2), "near")

    @when(not_quad)
    def _():
        mirror = jnp.where(zd % 4 < 2, 3, 0)
        rank = (z % 4) ^ mirror
        base = (z // 4) * 4

        def onward(target, slot, name, cond):
            bpb[...] = bpart[...].astype(BF)
            send(bpb, tb.at[slot], cond, name, dev(q, k, base + (target ^ mirror)), 6)

        @when(rank % 2 == 1)
        def _():
            onward(rank - 1, 0, "tr1", "odd")

        @when(rank % 2 == 0)
        def _():
            wait(tb.at[0], "tr1")
            bpart[...] += tb[0].astype(F32)

        @when(rank == 2)
        def _():
            onward(0, 1, "tr2", "two")

        @when(rank == 0)
        def _():
            wait(tb.at[1], "tr2")
            bpart[...] += tb[1].astype(F32)
            to_diag(3, "exit")

    @when(diag)
    def _():
        def rest(w):
            wait(fb.at[w], "fb%d" % w)
            value = own(yo, w).astype(F32) - bpart[pl.ds(w * 256, 256), :]
            for i in range(4):
                value -= fb[w, pl.ds(i * 256, 256), :].astype(F32)
            return value

        keep(xo, 2, rest(2), uib)
        send(own_at(xo, 2), rows(xc2, place, 256, 256), "diag", "cx2", dev(q ^ 1, k, z), 2)
        put(xc2, place, 256, own(xo, 2))
        publish(xo, 2, os, "os", "diag")
        r1 = rest(1)
        acc[...] = rest(0)
        wait(yt4.at[pl.ds(0, 1280)], "s_ud")
        wait(xc2.at[pl.ds(0, 256)], "cx2")
        keep(xo, 1, r1 - dot(u12[...], xc2[...]), uib)
        publish(xo, 1, os, "os", "diag")
        keep(xo, 0, acc[...] - dot(u02[...], xc2[...]) - dot(u01[...], own(xo, 1)), uib)
        publish(xo, 0, os, "os", "diag")

    wait(of, "of")
    wait(os, "os")

    @when(both(is_top, quad))
    def _():
        wait(yt4.at[pl.ds(0, 12 * 128)], "snd_x4")

    @when(both(is_top, not_quad))
    def _():
        wait(yt4.at[pl.ds(0, 16 * 128)], "snd_x4")

    rank = (z % 4) ^ jnp.where(zd % 4 < 2, 3, 0)
    where = {
        "all": None, "diag": diag, "ntop": not_top, "quad": quad, "quad_ntop": both(quad, not_top),
        "quad_top": both(quad, is_top), "pair_ntop": both(pair, not_top), "top": is_top, "top_far": far, "pair": pair,
        "npair": not_pair, "npair2": not_pair, "odd": both(not_quad, rank % 2 == 1), "two": both(not_quad, rank == 2),
        "exit": both(not_quad, rank == 0), "near": both(quad, not_diag),
    }
    for cond, units in sent.items():
        def drain(cond=cond, units=units):
            left = int(units * 128)
            while left > 0:
                now = min(left, 4096)
                wait(yt4.at[pl.ds(0, now)], "snd_" + cond)
                left -= now

        if where[cond] is None:
            drain()
        else:
            when(where[cond])(drain)


def on_device(right_side, l_factor, u_factor, l_pattern, u_pattern, l_inverse, u_inverse):
    vm = lambda *shape: pltpu.VMEM(shape, BF)
    anywhere = pl.BlockSpec(memory_space=pl.ANY)
    scratch = [
        pltpu.SMEM((6, 24), jnp.int32), pltpu.SMEM((6, 24), jnp.int32),
        vm(2, 768, 128), vm(2, 6, 128, 128), vm(2, 6, 128, 128),
        vm(640, 3072), vm(640, 3072),
        vm(256, 256), vm(256, 1024), vm(768, 2048), vm(768, 1536), vm(256, 512), vm(256, 512), vm(256, 256),
        vm(256, 512), vm(384, 512),
        vm(256, 2048), vm(256, 4096), vm(256, 4096), vm(256, 2048), vm(256, 4096),
        vm(1536, 128), vm(1536, 128), vm(1536, 128), vm(768, 128),
        vm(512, 128), vm(1024, 128), vm(2048, 128),
        vm(4096, 128), vm(4096, 128), vm(4096, 128), vm(2048, 128),
        vm(512, 128), vm(512, 128), vm(512, 128), vm(512, 128),
        pltpu.VMEM((256, 128), F32), pltpu.VMEM((768, 128), F32), vm(768, 128),
        vm(3, 1024, 128), vm(2, 768, 128), vm(512, 128),
        pltpu.SemaphoreType.DMA((len(SEM),)),
    ]
    return pl.pallas_call(
        kernel,
        out_shape=(jax.ShapeDtypeStruct((768, 256), BF), jax.ShapeDtypeStruct((768, 256), BF)),
        in_specs=[anywhere] * 7,
        out_specs=(anywhere, anywhere),
        scratch_shapes=scratch,
        compiler_params=pltpu.CompilerParams(collective_id=0, has_side_effects=True, vmem_limit_bytes=VMEM_LIMIT),
        name="sweeps",
    )(right_side, l_factor, u_factor, l_pattern, u_pattern, l_inverse, u_inverse)


def solution(mesh):
    placed = (
        P("prow", None),
        P("prow", "pcol"),
        P("prow", "pcol"),
        P("prow", "pcol"),
        P("prow", "pcol"),
        P("prow", None, None),
        P("prow", None, None),
    )
    return jax.shard_map(
        on_device,
        mesh=mesh,
        in_specs=placed,
        out_specs=(P("prow", None), P("prow", None)),
        check_vma=False,
    )
```

```python
import jax
import jax.numpy as jnp
from jax import lax
from jax.experimental import pallas as pl
from jax.experimental.pallas import tpu as pltpu
from jax.sharding import PartitionSpec as P

MESH = pl.DeviceIdType.MESH
BF = jnp.bfloat16
F32 = jnp.float32
VMEM_LIMIT = 62 * 2**20

class N:
    (
        rhs, li, ui, lp, up, l1, l2, l3, l4, l5, u0, u1, u2, u3, u4, s_rhs, s_li, s_ui, s_l1, s_l2, s_lb, s_ub, s_ud,
        y0, y1, y2, sc, ag, sc2, ag2, y3, f3, f4, f5, t43, t54, t45, t34, t35, ty3a, ty3b, ty4, tx5, tx4, x5, x4, x3,
        sd0, sd1, sd2, tr10, tr11, tr12, tr20, tr21, tr22, fb0, fb1, fb2, cx2, of, os, xl, c_all, c_diag, c_ntop,
        c_quad, c_quad_ntop, c_quad_top, c_pair_ntop, c_top, c_top_far, c_x4, c_spread, c_pair, c_npair, c_npair2,
        c_u45, c_sidefar, c_leaf, c_leaf1, c_mid, c_exit, c_near, c_side,
    ) = range(85)


def dot(a, b):
    return jnp.dot(a, b, preferred_element_type=F32)


def kernel(
    rhs, lf, uf, lph, uph, li, ui, of, os,
    lp, up, rb, lib, uib, ls, us, l1b, l2b, lb, ub, u12, u02, u01,
    mtl, mtu, lt43, lt54, ut45, ut34, ut35,
    yo, xo, yb, part, f3, f4, f5, yt3, yt4, xt5, xt4, xb5, xb4, xb3, yb3, acc, bpart, bpb, fb, tb, xc2,
    sem,
):
    p = lax.axis_index("prow")
    z = lax.axis_index("pcol")
    q, k = p // 2, p % 2
    zd = q // 2
    half = q % 2
    top = 1 + 4 * k
    other_top = 5 - 4 * k
    block_row = z // 2
    diag = z == zd
    pair = block_row == q // 4
    quad = z // 4 == q // 8
    is_top = z == top
    not_top = z != top
    not_diag = z != zd
    not_pair = block_row != q // 4
    not_quad = z // 4 != q // 8
    me = pl.multiple_of(k * 128, 128)
    both = jnp.logical_and

    def S(name):
        return sem.at[name]

    def dev(qq, kk, zz):
        return (qq * 2 + kk, zz)

    sent = {}

    def send_raw(src, dst, cond, rsem, device):
        pltpu.make_async_remote_copy(
            src_ref=src, dst_ref=dst, send_sem=S(cond), recv_sem=S(rsem), device_id=device, device_id_type=MESH
        ).start()

    def send(src, dst, cond, rsem, device, units):
        send_raw(src, dst, cond, rsem, device)
        sent[cond] = sent.get(cond, 0) + units

    def local(src, dst, s):
        pltpu.make_async_copy(src, dst, S(s)).start()

    def wait(ref, s):
        pltpu.make_async_copy(ref, ref, S(s)).wait()

    def rows(ref, start, size, align=128):
        return ref.at[pl.ds(pl.multiple_of(start, align), size)]

    when = pl.when
    sib = dev(q, 1 - k, z)

    bar = pltpu.get_barrier_semaphore()

    def hello(device):
        pl.semaphore_signal(bar, inc=1, device_id=device, device_id_type=MESH)

    for d in range(1, 16):
        hello(dev(q ^ d, k, z))
    for j in range(1, 8):
        hello(dev(q, k, (z + j) % 8))
    for j in range(8):
        hello(dev(q, 1 - k, (z + j) % 8))
    far = both(is_top, zd != top)
    near = both(not_top, pair)
    near_diag = both(near, diag)
    near_rest = both(near, not_diag)

    @when(far)
    def _():
        for d in range(1, 4):
            hello(dev(q ^ d, k, zd))

    @when(near_diag)
    def _():
        hello(dev(q ^ 1, k, top))

    @when(near_rest)
    def _():
        hello(dev(2 * z, k, top))
        hello(dev(2 * z + 1, k, top))

    local(rhs.at[:, pl.ds(me, 128)], rb.at[k], N.rhs)
    local(li, lib.at[k], N.li)
    local(lph, lp, N.lp)
    local(uph, up, N.up)

    @when(diag)
    def _():
        for v in (1, 2):
            local(lf.at[pl.ds(v * 128, 128), :], ls.at[pl.ds((v - 1) * 128, 128), :], N.l1 + v - 1)

    for v in (4, 5, 3):
        local(lf.at[pl.ds(v * 128, 128), :], ls.at[pl.ds((v - 1) * 128, 128), :], N.l1 + v - 1)
    local(ui, uib.at[k], N.ui)
    for w in (4, 3, 0, 1, 2):
        local(uf.at[pl.ds(w * 128, 128), :], us.at[pl.ds(w * 128, 128), :], N.u0 + w)

    def mask(stage, pattern, srow, prow, col, dst, drow, dcol):
        block = stage[pl.ds(srow, 128), pl.ds(pl.multiple_of(col * 128, 128), 128)]
        keep = jnp.full((128, 128), pattern[prow, col].astype(F32)).astype(BF)
        dst[pl.ds(pl.multiple_of(drow, 128), 128), pl.ds(pl.multiple_of(dcol, 128), 128)] = block * keep

    def each_group(body):
        def step(j, carry):
            body(j)
            return carry

        lax.fori_loop(0, 4, step, 0)

    def each_own(body):
        for j2 in range(2):
            body(j2, 2 * half + j2)

    pltpu.make_async_copy(lph, lp, S(N.lp)).wait()
    pltpu.make_async_copy(uph, up, S(N.up)).wait()

    @when(diag)
    def _():
        wait(ls.at[pl.ds(0, 128), :], N.l1)
        each_own(lambda j2, j: mask(ls, lp, 0, 1, j * 6, l1b, me, j2 * 128))
        wait(ls.at[pl.ds(128, 128), :], N.l2)

        def level2(j):
            for w in range(2):
                mask(ls, lp, 128, 2, j * 6 + w, l2b, me, w * 512 + j * 128)

        each_group(level2)

    wait(ls.at[pl.ds(384, 128), :], N.l4)
    wait(ls.at[pl.ds(512, 128), :], N.l5)

    def lower_top(j):
        mask(ls, lp, 384, 4, j * 6 + 3, mtl, 0, j * 128)
        mask(ls, lp, 512, 5, j * 6 + 4, mtl, 128, j * 128)

    each_group(lower_top)

    for cond, count in ((far, 33), (near_diag, 31), (near_rest, 32)):
        @when(cond)
        def _(count=count):
            pl.semaphore_wait(bar, count)

    @when(jnp.logical_not(jnp.logical_or(far, near)))
    def _():
        pl.semaphore_wait(bar, 30)

    send(rhs.at[:, pl.ds(pl.multiple_of((1 - k) * 128, 128), 128)], rb.at[k], N.c_all, N.s_rhs, sib, 6)
    send(li, lib.at[k], N.c_all, N.s_li, sib, 6)

    @when(diag)
    def _():
        send(l1b.at[pl.ds(me, 128)], l1b.at[pl.ds(me, 128)], N.c_diag, N.s_l1, sib, 2)
        send(l2b.at[pl.ds(me, 128)], l2b.at[pl.ds(me, 128)], N.c_diag, N.s_l2, sib, 8)

    def to_top(src, dst, column, name, everywhere, tag=None):
        view = dst.at[pl.ds(me, 128), pl.ds(pl.multiple_of(column * 512, 512), 512)]

        def from_rest():
            cond = tag or (N.c_ntop if everywhere else N.c_quad_ntop)
            send(src, view, cond, name, dev(q, k, top), 4)
            send(src, view, cond, name, dev(q, 1 - k, other_top), 4)

        def from_top():
            local(src, view, name)
            send(src, view, N.c_top if everywhere else N.c_quad_top, name, dev(q, 1 - k, other_top), 4)

        for mine, go in ((not_top, from_rest), (is_top, from_top)):
            when(mine if everywhere else both(mine, quad))(go)

    to_top(mtl.at[pl.ds(0, 128)], lt43, z % 4, N.t43, False)
    to_top(mtl.at[pl.ds(128, 128)], lt54, z, N.t54, True)

    def solve(inverse, level, resid):
        for g in range(2):
            piece = resid[g * 128 : (g + 1) * 128].astype(BF)
            yield dot(inverse[g, level], piece).astype(BF)

    def right(level):
        return jnp.concatenate([rb[g, pl.ds(level * 128, 128), :] for g in range(2)], axis=0).astype(F32)

    def keep(store, level, resid, inverse):
        for g, value in enumerate(solve(inverse, level, resid)):
            store[pl.ds(level * 256 + g * 128, 128), :] = value

    def own(store, level):
        return store[pl.ds(level * 256, 256), :]

    def own_at(store, level):
        return store.at[pl.ds(level * 256, 256)]

    def put(ref, start, size, value):
        ref[pl.ds(pl.multiple_of(start, size), size), :] = value

    wait(rb.at[0], N.rhs)
    wait(lib.at[0], N.li)
    wait(rb.at[0], N.s_rhs)
    wait(lib.at[0], N.s_li)
    keep(yo, 0, right(0), lib)
    place = half * 256

    def spread(level):
        for d in range(1, 4 if level < 2 else 8):
            send(own_at(yo, level), rows(yb, level * 512 + place, 256), N.c_diag, N.y0 + level, dev(q ^ d, k, z), 2)

    @when(diag)
    def _():
        spread(0)
        wait(l1b.at[pl.ds(0, 128)], N.s_l1)
        keep(yo, 1, right(1) - dot(l1b[...], own(yo, 0)), lib)
        spread(1)
        put(yb, place, 256, own(yo, 0))
        put(yb, 512 + place, 256, own(yo, 1))

    wait(ls.at[pl.ds(256, 128), :], N.l3)
    for v in (3, 4, 5):
        def low(j, v=v):
            for w in range(3 if v < 5 else 4):
                mask(ls, lp, (v - 1) * 128, v, j * 6 + w, lb, (v - 3) * 256 + me, w * 512 + j * 128)

        each_group(low)
        width = 1536 if v < 5 else 2048
        mine = lb.at[pl.ds(pl.multiple_of((v - 3) * 256 + me, 128), 128), pl.ds(0, width)]
        send(mine, mine, N.c_all, N.s_lb, sib, width // 128)

    @when(diag)
    def _():
        wait(l2b.at[pl.ds(0, 128)], N.s_l2)
        wait(yb.at[pl.ds(0, 256)], N.y0)
        wait(yb.at[pl.ds(0, 256)], N.y1)
        keep(yo, 2, right(2) - dot(l2b[...], yb[pl.ds(0, 1024), :]), lib)
        spread(2)
        put(yb, 1024 + place, 256, own(yo, 2))

    wait(us.at[pl.ds(512, 128), :], N.u4)
    each_group(lambda j: mask(us, up, 512, 4, j * 6 + 5, mtu, 0, j * 128))
    wait(us.at[pl.ds(384, 128), :], N.u3)

    def upper3(j):
        mask(us, up, 384, 3, j * 6 + 4, mtu, 128, j * 128)
        mask(us, up, 384, 3, j * 6 + 5, mtu, 256, j * 128)

    each_group(upper3)
    wait(uib.at[0], N.ui)
    send(uib.at[k], uib.at[k], N.c_all, N.s_ui, sib, 6)
    def fold_at(level):
        return pl.ds((level - 3) * 256, 256)

    def fold_here(level, dst, slot):
        put(dst, slot * 256, 256, part[fold_at(level), :])

    def fold_there(level, dst, slot, cond, name):
        send(part.at[fold_at(level)], rows(dst, slot * 256, 256), cond, name, dev(q, k, top), 2)

    def low_part(level):
        return dot(lb[fold_at(level), pl.ds(0, 1536)], yb[...])

    wait(lb.at[pl.ds(0, 320)], N.s_lb)

    def piece(owner):
        return rows(yb, owner * 64, 64, 64)

    @when(both(pair, not_diag))
    def _():
        wait(yb.at[pl.ds(0, 512)], N.y0)
        wait(yb.at[pl.ds(0, 512)], N.y1)

    @when(pair)
    def _():
        for d in (4, 8, 12):
            send(piece(q ^ d), piece(q ^ d), N.c_pair, N.sc, dev(q ^ d, k, z), 1 / 2)
        for d in range(4, 16):
            send(piece(q), piece(q), N.c_pair, N.ag, dev(q ^ d, k, z), 1 / 2)

    @when(not_pair)
    def _():
        wait(yb.at[pl.ds(0, 64)], N.sc)
        for d in range(1, 4):
            send(piece(q), piece(q), N.c_npair, N.ag, dev(q ^ d, k, z), 1 / 2)
        for e in range(1, 4):
            @when((q // 4) ^ e != block_row)
            def _(e=e):
                for d in range(4 * e, 4 * e + 4):
                    send_raw(piece(q), piece(q), N.c_npair2, N.ag, dev(q ^ d, k, z))

    sent[N.c_npair2] = 4
    for w in range(3):
        wait(us.at[pl.ds(w * 128, 128), :], N.u0 + w)

        def high(j, w=w):
            for v in (3, 4, 5):
                mask(us, up, w * 128, w, j * 6 + v, ub, w * 256 + me, (v - 3) * 512 + j * 128)

        each_group(high)
        mine = rows(ub, w * 256 + me, 128)
        send(mine, mine, N.c_all, N.s_ub, sib, 12)

    @when(diag)
    def _():
        def near_columns(j):
            mask(us, up, 128, 1, j * 6 + 2, u12, me, j * 128)
            mask(us, up, 0, 0, j * 6 + 2, u02, me, j * 128)

        each_group(near_columns)
        each_own(lambda j2, j: mask(us, up, 0, 0, j * 6 + 1, u01, me, j2 * 128))
        for ref, units in ((u12, 4), (u02, 4), (u01, 2)):
            send(ref.at[pl.ds(me, 128)], ref.at[pl.ds(me, 128)], N.c_diag, N.s_ud, sib, units)

    @when(diag)
    def _():
        wait(yb.at[pl.ds(0, 256)], N.y2)

    @when(both(quad, not_diag))
    def _():
        wait(yb.at[pl.ds(0, 512)], N.y2)

    @when(not_pair)
    def _():
        wait(yb.at[pl.ds(0, 15 * 64)], N.ag)

    def fold(level, dst, slot, cond, name):
        part[fold_at(level), :] = low_part(level).astype(BF)

        @when(is_top)
        def _():
            fold_here(level, dst, slot)

        @when(not_top)
        def _():
            fold_there(level, dst, slot, cond, name)

    @when(pair)
    def _():
        fold(3, f3, z % 2, N.c_pair_ntop, N.f3)

    eighth = rows(yb, 1024 + (q % 8) * 64, 64, 64)

    @when(quad)
    def _():
        fold(4, f4, z % 4, N.c_quad_ntop, N.f4)
        send(eighth, eighth, N.c_quad, N.sc2, dev(q ^ 8, k, z), 1 / 2)

    def total(ref, count):
        value = ref[pl.ds(0, 256), :].astype(F32)
        for i in range(1, count):
            value += ref[pl.ds(i * 256, 256), :].astype(F32)
        return value

    @when(is_top)
    def _():
        @when(pair)
        def _():
            wait(f3.at[pl.ds(0, 256)], N.f3)

        @when(not_pair)
        def _():
            wait(f3, N.f3)

        keep(yo, 3, right(3) - total(f3, 2), lib)
        for d in range(1, 8):
            send(own_at(yo, 3), rows(yt3, q * 256, 256, 256), N.c_top, N.ty3a, dev(q ^ d, k, z), 2)
        for d in range(8, 16):
            send(own_at(yo, 3), rows(yt3, q * 256, 256, 256), N.c_top, N.ty3b, dev(q ^ d, k, z), 2)
        put(yt3, q * 256, 256, own(yo, 3))

    @when(not_quad)
    def _():
        wait(yb.at[pl.ds(0, 64)], N.sc2)
        for d in range(1, 8):
            send(eighth, eighth, N.c_spread, N.ag2, dev(q ^ d, k, z), 1 / 2)
        wait(yb.at[pl.ds(0, 7 * 64)], N.ag2)

    acc[...] = low_part(5)

    to_top(mtu.at[pl.ds(0, 128)], ut45, z, N.t45, True, N.c_u45)

    def sum5():
        mixed = acc[...] + dot(lb[fold_at(5), pl.ds(1536, 512)], yb3[...])
        part[fold_at(5), :] = mixed.astype(BF)

    @when(not_top)
    def _():
        wait(yb3, N.y3)
        sum5()
        fold_there(5, f5, z, N.c_ntop, N.f5)

    def publish(store, level, out, name, cond):
        dst = out.at[pl.ds(level * 128, 128), pl.ds(me, 128)]
        for flip in (0, 1):
            core = (k + flip) % 2
            src = rows(store, level * 256 + core * 128, 128)
            for j in range(8):
                if flip == 0 and j == 0:
                    local(src, dst, name)
                else:
                    send(src, dst, cond, name, dev(q, core, (z + j) % 8), 1)

    out0 = of.at[pl.ds(0, 128), pl.ds(me, 128)]
    local(rows(yo, me, 128), out0, N.of)
    send(rows(yo, pl.multiple_of((1 - k) * 128, 128), 128), out0, N.c_all, N.of, sib, 1)
    wait(uib.at[0], N.s_ui)

    @when(not_top)
    def _():
        wait(yt4.at[pl.ds(0, 8 * 128)], N.c_u45)

    to_top(mtu.at[pl.ds(128, 128)], ut34, z % 4, N.t34, False)
    to_top(mtu.at[pl.ds(256, 128)], ut35, z, N.t35, True)

    @when(diag)
    def _():
        publish(yo, 1, of, N.of, N.c_diag)
        publish(yo, 2, of, N.of, N.c_diag)

    order = (2, 1, 0)

    def add_up(w, columns, x, first=False):
        here = pl.ds(w * 256, 256)
        value = dot(ub[here, pl.ds(columns, 512)], x[...])
        bpart[here, :] = value if first else bpart[here, :] + value

    def to_diag(w, slot, cond):
        here = pl.ds(w * 256, 256)
        bpb[here, :] = bpart[here, :].astype(BF)
        send(bpb.at[here], fb.at[w, pl.ds(pl.multiple_of(slot * 256, 256), 256)], cond, N.fb0 + w, dev(q, k, zd), 2)

    high = zd % 4 < 2
    low_end = zd % 4 >= 2
    turn = z % 4
    base = (z // 4) * 4

    def onward(w, target, slot, cond):
        here = pl.ds(w * 256, 256)
        bpb[here, :] = bpart[here, :].astype(BF)
        send(bpb.at[here], tb.at[slot, here], cond, ((N.tr10, N.tr11, N.tr12), (N.tr20, N.tr21, N.tr22))[slot][w], dev(q, k, base + target), 2)

    def take(w, slot):
        here = pl.ds(w * 256, 256)
        wait(tb.at[slot, here], ((N.tr10, N.tr11, N.tr12), (N.tr20, N.tr21, N.tr22))[slot][w])
        bpart[here, :] += tb[slot, here, :].astype(F32)

    def leaf_one():
        for w in order:
            add_up(w, 1024, xb5, True)
            onward(w, jnp.where(high, 2, 0), 1, N.c_leaf1)

    is_end = turn == jnp.where(high, 3, 0)
    is_leaf = turn == jnp.where(high, 0, 3)

    @when(is_top)
    def _():
        wait(yt3.at[pl.ds(0, 7 * 256)], N.ty3a)
        wait(yt3.at[pl.ds(0, 8 * 256)], N.ty3b)
        for j in range(1, 8):
            zz = (z + j) % 8
            send(rows(yt3, zz * 512, 512, 512), yb3, N.c_top, N.y3, dev(q, k, zz), 4)
        yb3[...] = yt3[pl.ds(pl.multiple_of(z * 512, 512), 512), :]

        @when(quad)
        def _():
            wait(f4.at[pl.ds(0, 768)], N.f4)

        @when(not_quad)
        def _():
            wait(f4, N.f4)

        s4 = right(4) - total(f4, 4)
        wait(lt43, N.t43)
        eight = pl.ds(pl.multiple_of((q // 8) * 2048, 2048), 2048)
        keep(yo, 4, s4 - dot(lt43[...], yt3[eight, :]), lib)
        for d in range(1, 16):
            send(own_at(yo, 4), rows(yt4, q * 256, 256, 256), N.c_top, N.ty4, dev(q ^ d, k, z), 2)
        put(yt4, q * 256, 256, own(yo, 4))
        sum5()
        fold_here(5, f5, z)
        publish(yo, 3, of, N.of, N.c_top)
        wait(f5.at[pl.ds(0, 7 * 256)], N.f5)
        acc[...] = right(5) - total(f5, 8)
        wait(lt54, N.t54)
        wait(yt4.at[pl.ds(0, 15 * 256)], N.ty4)
        keep(yo, 5, acc[...] - dot(lt54[...], yt4[...]), lib)
        keep(xo, 5, own(yo, 5).astype(F32), uib)
        for d in range(1, 16):
            send(own_at(xo, 5), rows(xt5, q * 256, 256, 256), N.c_top, N.tx5, dev(q ^ d, k, z), 2)
        put(xt5, q * 256, 256, own(xo, 5))
        publish(yo, 4, of, N.of, N.c_top)
        wait(ut45, N.t45)
        wait(xt5.at[pl.ds(0, 15 * 256)], N.tx5)
        keep(xo, 4, own(yo, 4).astype(F32) - dot(ut45[...], xt5[...]), uib)
        for d in range(1, 8):
            send(own_at(xo, 4), rows(xt4, (q % 8) * 256, 256, 256), N.c_top, N.tx4, dev(q ^ d, k, z), 2)
        put(xt4, (q % 8) * 256, 256, own(xo, 4))
        for j in range(8):
            zz = (4 - (q // 8) * 4 + j) % 8

            @when(zz != z)
            def _(zz=zz):
                send_raw(rows(xt5, zz * 512, 512, 512), xb5, N.c_top, N.x5, dev(q, k, zz))

        sent[N.c_top] += 28
        xb5[...] = xt5[pl.ds(pl.multiple_of(z * 512, 512), 512), :]

        @when(not_quad)
        def _():
            wait(ub.at[pl.ds(0, 384)], N.s_ub)
            leaf_one()

        wait(ut35, N.t35)
        acc[...] = own(yo, 3).astype(F32) - dot(ut35[...], xt5[...])
        wait(xt4.at[pl.ds(0, 7 * 256)], N.tx4)

        for j in range(4):
            zz = (q // 8) * 4 + j
            src = rows(xt4, j * 512, 512, 512)

            @when(zz == z)
            def _(src=src):
                local(src, xb4, N.xl)
                wait(xb4, N.xl)

            @when(zz != z)
            def _(src=src, zz=zz):
                send_raw(src, xb4, N.c_x4, N.x4, dev(q, k, zz))

        wait(ut34, N.t34)
        keep(xo, 3, acc[...] - dot(ut34[...], xt4[...]), uib)
        at = rows(xb3, half * 256, 256, 256)
        for d in range(1, 4):
            @when(zd == top)
            def _(d=d):
                send_raw(own_at(xo, 3), at, N.c_top, N.x3, dev(q ^ d, k, z))

            @when(zd != top)
            def _(d=d):
                send_raw(own_at(xo, 3), at, N.c_top, N.x3, dev(q ^ d, k, zd))

        sent[N.c_top] += 6

        @when(zd == top)
        def _():
            put(xb3, half * 256, 256, own(xo, 3))

        @when(zd != top)
        def _():
            send(own_at(xo, 3), at, N.c_top_far, N.x3, dev(q, k, zd), 2)

    @when(jnp.logical_or(not_top, quad))
    def _():
        wait(ub.at[pl.ds(0, 384)], N.s_ub)

    @when(not_top)
    def _():
        wait(xb5, N.x5)

    @when(not_quad)
    def _():
        @when(both(turn == 1, not_top))
        def _():
            leaf_one()
            sent[N.c_leaf1] = 6

        @when(is_leaf)
        def _():
            for w in order:
                add_up(w, 1024, xb5, True)
                onward(w, 2, 0, N.c_leaf)

        @when(turn == 2)
        def _():
            for w in order:
                add_up(w, 1024, xb5, True)
            for w in order:
                take(w, 0)

                @when(high)
                def _(w=w):
                    take(w, 1)

                onward(w, jnp.where(high, 3, 0), 0, N.c_mid)

        @when(is_end)
        def _():
            for w in order:
                add_up(w, 1024, xb5, True)
            for w in order:
                take(w, 0)

                @when(low_end)
                def _(w=w):
                    take(w, 1)

                to_diag(w, 2, N.c_exit)

    @when(quad)
    def _():
        for w in order:
            add_up(w, 1024, xb5, True)

        @when(not_top)
        def _():
            wait(xb4, N.x4)

        @when(pair)
        def _():
            for w in order:
                add_up(w, 512, xb4)
            mine_too = both(is_top, diag)

            @when(mine_too)
            def _():
                wait(xb3.at[pl.ds(0, 256)], N.x3)

            @when(jnp.logical_not(mine_too))
            def _():
                wait(xb3, N.x3)

            for w in order:
                add_up(w, 0, xb3)

                @when(not_diag)
                def _(w=w):
                    to_diag(w, 0, N.c_near)

        @when(not_pair)
        def _():
            close = jnp.logical_or(z % 4 == 1, z % 4 == 2)

            @when(jnp.logical_not(close))
            def _():
                for w in order:
                    add_up(w, 512, xb4)
                    here = pl.ds(w * 256, 256)
                    bpb[here, :] = bpart[here, :].astype(BF)
                    send(bpb.at[here], tb.at[0, here], N.c_sidefar, N.sd0 + w, dev(q, k, z ^ 1), 2)

            @when(close)
            def _():
                for w in order:
                    add_up(w, 512, xb4)
                    here = pl.ds(w * 256, 256)
                    wait(tb.at[0, here], N.sd0 + w)
                    bpart[here, :] += tb[0, here, :].astype(F32)
                    to_diag(w, 1, N.c_side)

    @when(diag)
    def _():
        def rest(w):
            wait(fb.at[w], N.fb0 + w)
            value = own(yo, w).astype(F32) - bpart[pl.ds(w * 256, 256), :]
            for i in range(3):
                value -= fb[w, pl.ds(i * 256, 256), :].astype(F32)
            return value

        keep(xo, 2, rest(2), uib)
        send(own_at(xo, 2), rows(xc2, place, 256, 256), N.c_diag, N.cx2, dev(q ^ 1, k, z), 2)
        put(xc2, place, 256, own(xo, 2))
        publish(xo, 2, os, N.os, N.c_diag)
        r1 = rest(1)
        acc[...] = rest(0)
        wait(yt4.at[pl.ds(0, 1280)], N.s_ud)
        wait(xc2.at[pl.ds(0, 256)], N.cx2)
        keep(xo, 1, r1 - dot(u12[...], xc2[...]), uib)
        publish(xo, 1, os, N.os, N.c_diag)
        keep(xo, 0, acc[...] - dot(u02[...], xc2[...]) - dot(u01[...], own(xo, 1)), uib)
        publish(xo, 0, os, N.os, N.c_diag)

    @when(is_top)
    def _():
        publish(yo, 5, of, N.of, N.c_top)
        for level in (5, 4, 3):
            publish(xo, level, os, N.os, N.c_top)

    wait(of, N.of)
    wait(os, N.os)

    @when(both(is_top, quad))
    def _():
        wait(yt4.at[pl.ds(0, 12 * 128)], N.c_x4)

    @when(both(is_top, not_quad))
    def _():
        wait(yt4.at[pl.ds(0, 16 * 128)], N.c_x4)

    where = {
        N.c_all: None, N.c_diag: diag, N.c_ntop: not_top, N.c_quad: quad, N.c_quad_ntop: both(quad, not_top),
        N.c_quad_top: both(quad, is_top), N.c_pair_ntop: both(pair, not_top), N.c_top: is_top, N.c_top_far: far, N.c_spread: not_quad,
        N.c_leaf: both(not_quad, is_leaf), N.c_leaf1: both(not_quad, turn == 1), N.c_mid: both(not_quad, turn == 2),
        N.c_exit: both(not_quad, is_end), N.c_near: both(pair, not_diag),
        N.c_side: both(both(quad, not_pair), jnp.logical_or(z % 4 == 1, z % 4 == 2)),
        N.c_sidefar: both(both(quad, not_pair), jnp.logical_or(z % 4 == 0, z % 4 == 3)),
        N.c_pair: pair, N.c_npair: not_pair, N.c_npair2: not_pair,
    }
    del sent[N.c_u45]
    for cond, units in sent.items():
        def drain(cond=cond, units=units):
            left = int(units * 128)
            while left > 0:
                now = min(left, 4096)
                wait(yt4.at[pl.ds(0, now)], cond)
                left -= now

        if where[cond] is None:
            drain()
        else:
            when(where[cond])(drain)


def on_device(right_side, l_factor, u_factor, l_pattern, u_pattern, l_inverse, u_inverse):
    vm = lambda *shape: pltpu.VMEM(shape, BF)
    anywhere = pl.BlockSpec(memory_space=pl.ANY)
    scratch = [
        pltpu.SMEM((6, 24), jnp.int32), pltpu.SMEM((6, 24), jnp.int32),
        vm(2, 768, 128), vm(2, 6, 128, 128), vm(2, 6, 128, 128),
        vm(640, 3072), vm(640, 3072),
        vm(256, 256), vm(256, 1024), vm(768, 2048), vm(768, 1536), vm(256, 512), vm(256, 512), vm(256, 256),
        vm(256, 512), vm(384, 512),
        vm(256, 2048), vm(256, 4096), vm(256, 4096), vm(256, 2048), vm(256, 4096),
        vm(1536, 128), vm(1536, 128), vm(1536, 128), vm(768, 128),
        vm(512, 128), vm(1024, 128), vm(2048, 128),
        vm(4096, 128), vm(4096, 128), vm(4096, 128), vm(2048, 128),
        vm(512, 128), vm(512, 128), vm(512, 128), vm(512, 128),
        pltpu.VMEM((256, 128), F32), pltpu.VMEM((768, 128), F32), vm(768, 128),
        vm(3, 768, 128), vm(2, 768, 128), vm(512, 128),
        pltpu.SemaphoreType.DMA((85,)),
    ]
    return pl.pallas_call(
        kernel,
        out_shape=(jax.ShapeDtypeStruct((768, 256), BF), jax.ShapeDtypeStruct((768, 256), BF)),
        in_specs=[anywhere] * 7,
        out_specs=(anywhere, anywhere),
        scratch_shapes=scratch,
        compiler_params=pltpu.CompilerParams(collective_id=0, has_side_effects=True, vmem_limit_bytes=VMEM_LIMIT),
        name="sweeps",
    )(right_side, l_factor, u_factor, l_pattern, u_pattern, l_inverse, u_inverse)


def solution(mesh):
    placed = (
        P("prow", None),
        P("prow", "pcol"),
        P("prow", "pcol"),
        P("prow", "pcol"),
        P("prow", "pcol"),
        P("prow", None, None),
        P("prow", None, None),
    )
    return jax.shard_map(
        on_device,
        mesh=mesh,
        in_specs=placed,
        out_specs=(P("prow", None), P("prow", None)),
        check_vma=False,
    )
```

```python
import jax
import jax.numpy as jnp
from jax import lax
from jax.experimental import pallas as pl
from jax.experimental.pallas import tpu as pltpu
from jax.sharding import PartitionSpec as P

MESH = pl.DeviceIdType.MESH
BF = jnp.bfloat16
F32 = jnp.float32
VMEM_LIMIT = 62 * 2**20

class N:
    (
        rhs, li, ui, lp, up, l1, l2, l3, l4, l5, u0, u1, u2, u3, u4, s_rhs, s_li, s_ui, s_l1, s_l2, s_lb, s_ub, s_ud,
        y0, y1, y2, sc, ag, sc2, ag2, y3, f3, f4, f5, t43, t54, t45, t34, t35, ty3a, ty3b, ty4, tx5, tx4, x5, x4, x3,
        sd0, sd1, sd2, tr10, tr11, tr12, tr20, tr21, tr22, fb0, fb1, fb2, cx2, of, os, xl, c_all, c_diag, c_ntop,
        c_quad, c_quad_ntop, c_quad_top, c_pair_ntop, c_top, c_top_far, c_x4, c_spread, c_pair, c_npair, c_npair2,
        c_u45, c_sidefar, c_leaf, c_leaf1, c_mid, c_exit, c_near, c_side,
    ) = range(85)


def dot(a, b):
    return jnp.dot(a, b, preferred_element_type=F32)


def kernel(
    rhs, lf, uf, lph, uph, li, ui, of, os,
    lp, up, rb, lib, uib, ls, us, l1b, l2b, lb, ub, u12, u02, u01,
    mtl, mtu, lt43, lt54, ut45, ut34, ut35,
    yo, xo, yb, part, f3, f4, f5, yt3, yt4, xt5, xt4, xb5, xb4, xb3, yb3, acc, bpart, bpb, fb, tb, xc2,
    sem,
):
    p = lax.axis_index("prow")
    z = lax.axis_index("pcol")
    q, k = p // 2, p % 2
    zd = q // 2
    half = q % 2
    top = 1 + 4 * k
    other_top = 5 - 4 * k
    block_row = z // 2
    diag = z == zd
    pair = block_row == q // 4
    quad = z // 4 == q // 8
    is_top = z == top
    not_top = z != top
    not_diag = z != zd
    not_pair = block_row != q // 4
    not_quad = z // 4 != q // 8
    me = pl.multiple_of(k * 128, 128)
    both = jnp.logical_and

    def S(name):
        return sem.at[name]

    def dev(qq, kk, zz):
        return (qq * 2 + kk, zz)

    sent = {}

    def send_raw(src, dst, cond, rsem, device):
        pltpu.make_async_remote_copy(
            src_ref=src, dst_ref=dst, send_sem=S(cond), recv_sem=S(rsem), device_id=device, device_id_type=MESH
        ).start()

    def send(src, dst, cond, rsem, device, units):
        send_raw(src, dst, cond, rsem, device)
        sent[cond] = sent.get(cond, 0) + units

    def local(src, dst, s):
        pltpu.make_async_copy(src, dst, S(s)).start()

    def wait(ref, s):
        pltpu.make_async_copy(ref, ref, S(s)).wait()

    def rows(ref, start, size, align=128):
        return ref.at[pl.ds(pl.multiple_of(start, align), size)]

    when = pl.when
    sib = dev(q, 1 - k, z)

    bar = pltpu.get_barrier_semaphore()

    def hello(device):
        pl.semaphore_signal(bar, inc=1, device_id=device, device_id_type=MESH)

    for d in range(1, 16):
        hello(dev(q ^ d, k, z))
    for j in range(1, 8):
        hello(dev(q, k, (z + j) % 8))
    for j in range(8):
        hello(dev(q, 1 - k, (z + j) % 8))
    far = both(is_top, zd != top)
    near = both(not_top, pair)
    near_diag = both(near, diag)
    near_rest = both(near, not_diag)

    @when(far)
    def _():
        for d in range(1, 4):
            hello(dev(q ^ d, k, zd))

    @when(near_diag)
    def _():
        hello(dev(q ^ 1, k, top))

    @when(near_rest)
    def _():
        hello(dev(2 * z, k, top))
        hello(dev(2 * z + 1, k, top))

    local(rhs.at[:, pl.ds(me, 128)], rb.at[k], N.rhs)
    local(li, lib.at[k], N.li)
    local(lph, lp, N.lp)
    local(uph, up, N.up)

    @when(diag)
    def _():
        for v in (1, 2):
            local(lf.at[pl.ds(v * 128, 128), :], ls.at[pl.ds((v - 1) * 128, 128), :], N.l1 + v - 1)

    for v in (4, 5, 3):
        local(lf.at[pl.ds(v * 128, 128), :], ls.at[pl.ds((v - 1) * 128, 128), :], N.l1 + v - 1)
    local(ui, uib.at[k], N.ui)
    for w in (4, 3, 0, 1, 2):
        local(uf.at[pl.ds(w * 128, 128), :], us.at[pl.ds(w * 128, 128), :], N.u0 + w)

    def mask(stage, pattern, srow, prow, col, dst, drow, dcol):
        block = stage[pl.ds(srow, 128), pl.ds(pl.multiple_of(col * 128, 128), 128)]
        keep = jnp.full((128, 128), pattern[prow, col].astype(F32)).astype(BF)
        dst[pl.ds(pl.multiple_of(drow, 128), 128), pl.ds(pl.multiple_of(dcol, 128), 128)] = block * keep

    def each_group(body):
        def step(j, carry):
            body(j)
            return carry

        lax.fori_loop(0, 4, step, 0)

    def each_own(body):
        for j2 in range(2):
            body(j2, 2 * half + j2)

    pltpu.make_async_copy(lph, lp, S(N.lp)).wait()
    pltpu.make_async_copy(uph, up, S(N.up)).wait()

    @when(diag)
    def _():
        wait(ls.at[pl.ds(0, 128), :], N.l1)
        each_own(lambda j2, j: mask(ls, lp, 0, 1, j * 6, l1b, me, j2 * 128))
        wait(ls.at[pl.ds(128, 128), :], N.l2)

        def level2(j):
            for w in range(2):
                mask(ls, lp, 128, 2, j * 6 + w, l2b, me, w * 512 + j * 128)

        each_group(level2)

    wait(ls.at[pl.ds(384, 128), :], N.l4)
    wait(ls.at[pl.ds(512, 128), :], N.l5)

    def lower_top(j):
        mask(ls, lp, 384, 4, j * 6 + 3, mtl, 0, j * 128)
        mask(ls, lp, 512, 5, j * 6 + 4, mtl, 128, j * 128)

    each_group(lower_top)

    for cond, count in ((far, 33), (near_diag, 31), (near_rest, 32)):
        @when(cond)
        def _(count=count):
            pl.semaphore_wait(bar, count)

    @when(jnp.logical_not(jnp.logical_or(far, near)))
    def _():
        pl.semaphore_wait(bar, 30)

    send(rhs.at[:, pl.ds(pl.multiple_of((1 - k) * 128, 128), 128)], rb.at[k], N.c_all, N.s_rhs, sib, 6)
    send(li, lib.at[k], N.c_all, N.s_li, sib, 6)

    @when(diag)
    def _():
        send(l1b.at[pl.ds(me, 128)], l1b.at[pl.ds(me, 128)], N.c_diag, N.s_l1, sib, 2)
        send(l2b.at[pl.ds(me, 128)], l2b.at[pl.ds(me, 128)], N.c_diag, N.s_l2, sib, 8)

    def to_top(src, dst, column, name, everywhere, tag=None):
        view = dst.at[pl.ds(me, 128), pl.ds(pl.multiple_of(column * 512, 512), 512)]

        def from_rest():
            cond = tag or (N.c_ntop if everywhere else N.c_quad_ntop)
            send(src, view, cond, name, dev(q, k, top), 4)
            send(src, view, cond, name, dev(q, 1 - k, other_top), 4)

        def from_top():
            local(src, view, name)
            send(src, view, N.c_top if everywhere else N.c_quad_top, name, dev(q, 1 - k, other_top), 4)

        for mine, go in ((not_top, from_rest), (is_top, from_top)):
            when(mine if everywhere else both(mine, quad))(go)

    to_top(mtl.at[pl.ds(0, 128)], lt43, z % 4, N.t43, False)
    to_top(mtl.at[pl.ds(128, 128)], lt54, z, N.t54, True)

    def solve(inverse, level, resid):
        for g in range(2):
            piece = resid[g * 128 : (g + 1) * 128].astype(BF)
            yield dot(inverse[g, level], piece).astype(BF)

    def right(level):
        return jnp.concatenate([rb[g, pl.ds(level * 128, 128), :] for g in range(2)], axis=0).astype(F32)

    def keep(store, level, resid, inverse):
        for g, value in enumerate(solve(inverse, level, resid)):
            store[pl.ds(level * 256 + g * 128, 128), :] = value

    def own(store, level):
        return store[pl.ds(level * 256, 256), :]

    def own_at(store, level):
        return store.at[pl.ds(level * 256, 256)]

    def put(ref, start, size, value):
        ref[pl.ds(pl.multiple_of(start, size), size), :] = value

    wait(rb.at[0], N.rhs)
    wait(lib.at[0], N.li)
    wait(rb.at[0], N.s_rhs)
    wait(lib.at[0], N.s_li)
    keep(yo, 0, right(0), lib)
    place = half * 256

    def spread(level):
        for d in range(1, 4 if level < 2 else 8):
            send(own_at(yo, level), rows(yb, level * 512 + place, 256), N.c_diag, N.y0 + level, dev(q ^ d, k, z), 2)

    @when(diag)
    def _():
        spread(0)
        wait(l1b.at[pl.ds(0, 128)], N.s_l1)
        keep(yo, 1, right(1) - dot(l1b[...], own(yo, 0)), lib)
        spread(1)
        put(yb, place, 256, own(yo, 0))
        put(yb, 512 + place, 256, own(yo, 1))

    wait(ls.at[pl.ds(256, 128), :], N.l3)
    for v in (3, 4, 5):
        def low(j, v=v):
            for w in range(3 if v < 5 else 4):
                mask(ls, lp, (v - 1) * 128, v, j * 6 + w, lb, (v - 3) * 256 + me, w * 512 + j * 128)

        each_group(low)
        width = 1536 if v < 5 else 2048
        mine = lb.at[pl.ds(pl.multiple_of((v - 3) * 256 + me, 128), 128), pl.ds(0, width)]
        send(mine, mine, N.c_all, N.s_lb, sib, width // 128)

    @when(diag)
    def _():
        wait(l2b.at[pl.ds(0, 128)], N.s_l2)
        wait(yb.at[pl.ds(0, 256)], N.y0)
        wait(yb.at[pl.ds(0, 256)], N.y1)
        keep(yo, 2, right(2) - dot(l2b[...], yb[pl.ds(0, 1024), :]), lib)
        spread(2)
        put(yb, 1024 + place, 256, own(yo, 2))

    wait(us.at[pl.ds(512, 128), :], N.u4)
    each_group(lambda j: mask(us, up, 512, 4, j * 6 + 5, mtu, 0, j * 128))
    wait(us.at[pl.ds(384, 128), :], N.u3)

    def upper3(j):
        mask(us, up, 384, 3, j * 6 + 4, mtu, 128, j * 128)
        mask(us, up, 384, 3, j * 6 + 5, mtu, 256, j * 128)

    each_group(upper3)
    wait(uib.at[0], N.ui)
    send(uib.at[k], uib.at[k], N.c_all, N.s_ui, sib, 6)
    def fold_at(level):
        return pl.ds((level - 3) * 256, 256)

    def fold_here(level, dst, slot):
        put(dst, slot * 256, 256, part[fold_at(level), :])

    def fold_there(level, dst, slot, cond, name):
        send(part.at[fold_at(level)], rows(dst, slot * 256, 256), cond, name, dev(q, k, top), 2)

    def low_part(level):
        return dot(lb[fold_at(level), pl.ds(0, 1536)], yb[...])

    wait(lb.at[pl.ds(0, 320)], N.s_lb)

    def piece(owner):
        return rows(yb, owner * 64, 64, 64)

    @when(both(pair, not_diag))
    def _():
        wait(yb.at[pl.ds(0, 512)], N.y0)
        wait(yb.at[pl.ds(0, 512)], N.y1)

    @when(pair)
    def _():
        for d in (4, 8, 12):
            send(piece(q ^ d), piece(q ^ d), N.c_pair, N.sc, dev(q ^ d, k, z), 1 / 2)
        for d in range(4, 16):
            send(piece(q), piece(q), N.c_pair, N.ag, dev(q ^ d, k, z), 1 / 2)

    @when(not_pair)
    def _():
        wait(yb.at[pl.ds(0, 64)], N.sc)
        for d in range(1, 4):
            send(piece(q), piece(q), N.c_npair, N.ag, dev(q ^ d, k, z), 1 / 2)
        for e in range(1, 4):
            @when((q // 4) ^ e != block_row)
            def _(e=e):
                for d in range(4 * e, 4 * e + 4):
                    send_raw(piece(q), piece(q), N.c_npair2, N.ag, dev(q ^ d, k, z))

    sent[N.c_npair2] = 4
    for w in range(3):
        wait(us.at[pl.ds(w * 128, 128), :], N.u0 + w)

        def high(j, w=w):
            for v in (3, 4, 5):
                mask(us, up, w * 128, w, j * 6 + v, ub, w * 256 + me, (v - 3) * 512 + j * 128)

        each_group(high)
        mine = rows(ub, w * 256 + me, 128)
        send(mine, mine, N.c_all, N.s_ub, sib, 12)

    @when(diag)
    def _():
        def near_columns(j):
            mask(us, up, 128, 1, j * 6 + 2, u12, me, j * 128)
            mask(us, up, 0, 0, j * 6 + 2, u02, me, j * 128)

        each_group(near_columns)
        each_own(lambda j2, j: mask(us, up, 0, 0, j * 6 + 1, u01, me, j2 * 128))
        for ref, units in ((u12, 4), (u02, 4), (u01, 2)):
            send(ref.at[pl.ds(me, 128)], ref.at[pl.ds(me, 128)], N.c_diag, N.s_ud, sib, units)

    @when(diag)
    def _():
        wait(yb.at[pl.ds(0, 256)], N.y2)

    @when(both(quad, not_diag))
    def _():
        wait(yb.at[pl.ds(0, 512)], N.y2)

    @when(not_pair)
    def _():
        wait(yb.at[pl.ds(0, 15 * 64)], N.ag)

    def fold(level, dst, slot, cond, name):
        part[fold_at(level), :] = low_part(level).astype(BF)

        @when(is_top)
        def _():
            fold_here(level, dst, slot)

        @when(not_top)
        def _():
            fold_there(level, dst, slot, cond, name)

    @when(pair)
    def _():
        fold(3, f3, z % 2, N.c_pair_ntop, N.f3)

    eighth = rows(yb, 1024 + (q % 8) * 64, 64, 64)

    @when(quad)
    def _():
        fold(4, f4, z % 4, N.c_quad_ntop, N.f4)
        send(eighth, eighth, N.c_quad, N.sc2, dev(q ^ 8, k, z), 1 / 2)

    def total(ref, count):
        value = ref[pl.ds(0, 256), :].astype(F32)
        for i in range(1, count):
            value += ref[pl.ds(i * 256, 256), :].astype(F32)
        return value

    @when(is_top)
    def _():
        @when(pair)
        def _():
            wait(f3.at[pl.ds(0, 256)], N.f3)

        @when(not_pair)
        def _():
            wait(f3, N.f3)

        keep(yo, 3, right(3) - total(f3, 2), lib)
        for d in range(1, 8):
            send(own_at(yo, 3), rows(yt3, q * 256, 256, 256), N.c_top, N.ty3a, dev(q ^ d, k, z), 2)
        for d in range(8, 16):
            send(own_at(yo, 3), rows(yt3, q * 256, 256, 256), N.c_top, N.ty3b, dev(q ^ d, k, z), 2)
        put(yt3, q * 256, 256, own(yo, 3))

    @when(not_quad)
    def _():
        wait(yb.at[pl.ds(0, 64)], N.sc2)
        for d in range(1, 8):
            send(eighth, eighth, N.c_spread, N.ag2, dev(q ^ d, k, z), 1 / 2)
        wait(yb.at[pl.ds(0, 7 * 64)], N.ag2)

    acc[...] = low_part(5)

    to_top(mtu.at[pl.ds(0, 128)], ut45, z, N.t45, True, N.c_u45)
    to_top(mtu.at[pl.ds(128, 128)], ut34, z % 4, N.t34, False)

    def sum5():
        mixed = acc[...] + dot(lb[fold_at(5), pl.ds(1536, 512)], yb3[...])
        part[fold_at(5), :] = mixed.astype(BF)

    @when(not_top)
    def _():
        wait(yb3, N.y3)
        sum5()
        fold_there(5, f5, z, N.c_ntop, N.f5)

    def publish(store, level, out, name, cond):
        dst = out.at[pl.ds(level * 128, 128), pl.ds(me, 128)]
        for flip in (0, 1):
            core = (k + flip) % 2
            src = rows(store, level * 256 + core * 128, 128)
            for j in range(8):
                if flip == 0 and j == 0:
                    local(src, dst, name)
                else:
                    send(src, dst, cond, name, dev(q, core, (z + j) % 8), 1)

    out0 = of.at[pl.ds(0, 128), pl.ds(me, 128)]
    local(rows(yo, me, 128), out0, N.of)
    send(rows(yo, pl.multiple_of((1 - k) * 128, 128), 128), out0, N.c_all, N.of, sib, 1)
    wait(uib.at[0], N.s_ui)

    @when(not_top)
    def _():
        wait(yt4.at[pl.ds(0, 8 * 128)], N.c_u45)

    to_top(mtu.at[pl.ds(256, 128)], ut35, z, N.t35, True)

    @when(diag)
    def _():
        publish(yo, 1, of, N.of, N.c_diag)
        publish(yo, 2, of, N.of, N.c_diag)

    order = (2, 1, 0)

    def add_up(w, columns, x, first=False):
        here = pl.ds(w * 256, 256)
        value = dot(ub[here, pl.ds(columns, 512)], x[...])
        bpart[here, :] = value if first else bpart[here, :] + value

    def to_diag(w, slot, cond):
        here = pl.ds(w * 256, 256)
        bpb[here, :] = bpart[here, :].astype(BF)
        send(bpb.at[here], fb.at[w, pl.ds(pl.multiple_of(slot * 256, 256), 256)], cond, N.fb0 + w, dev(q, k, zd), 2)

    high = zd % 4 < 2
    low_end = zd % 4 >= 2
    turn = z % 4
    base = (z // 4) * 4

    def onward(w, target, slot, cond):
        here = pl.ds(w * 256, 256)
        bpb[here, :] = bpart[here, :].astype(BF)
        send(bpb.at[here], tb.at[slot, here], cond, ((N.tr10, N.tr11, N.tr12), (N.tr20, N.tr21, N.tr22))[slot][w], dev(q, k, base + target), 2)

    def take(w, slot):
        here = pl.ds(w * 256, 256)
        wait(tb.at[slot, here], ((N.tr10, N.tr11, N.tr12), (N.tr20, N.tr21, N.tr22))[slot][w])
        bpart[here, :] += tb[slot, here, :].astype(F32)

    def leaf_one():
        for w in order:
            add_up(w, 1024, xb5, True)
            onward(w, jnp.where(high, 2, 0), 1, N.c_leaf1)

    is_end = turn == jnp.where(high, 3, 0)
    is_leaf = turn == jnp.where(high, 0, 3)

    @when(is_top)
    def _():
        wait(yt3.at[pl.ds(0, 7 * 256)], N.ty3a)
        wait(yt3.at[pl.ds(0, 8 * 256)], N.ty3b)
        for j in range(1, 8):
            zz = (z + j) % 8
            send(rows(yt3, zz * 512, 512, 512), yb3, N.c_top, N.y3, dev(q, k, zz), 4)
        yb3[...] = yt3[pl.ds(pl.multiple_of(z * 512, 512), 512), :]

        @when(quad)
        def _():
            wait(f4.at[pl.ds(0, 768)], N.f4)

        @when(not_quad)
        def _():
            wait(f4, N.f4)

        s4 = right(4) - total(f4, 4)
        wait(lt43, N.t43)
        eight = pl.ds(pl.multiple_of((q // 8) * 2048, 2048), 2048)
        keep(yo, 4, s4 - dot(lt43[...], yt3[eight, :]), lib)
        for d in range(1, 16):
            send(own_at(yo, 4), rows(yt4, q * 256, 256, 256), N.c_top, N.ty4, dev(q ^ d, k, z), 2)
        put(yt4, q * 256, 256, own(yo, 4))
        sum5()
        fold_here(5, f5, z)
        publish(yo, 3, of, N.of, N.c_top)
        wait(f5.at[pl.ds(0, 7 * 256)], N.f5)
        acc[...] = right(5) - total(f5, 8)
        wait(lt54, N.t54)
        wait(yt4.at[pl.ds(0, 15 * 256)], N.ty4)
        keep(yo, 5, acc[...] - dot(lt54[...], yt4[...]), lib)
        keep(xo, 5, own(yo, 5).astype(F32), uib)
        for d in range(1, 16):
            send(own_at(xo, 5), rows(xt5, q * 256, 256, 256), N.c_top, N.tx5, dev(q ^ d, k, z), 2)
        put(xt5, q * 256, 256, own(xo, 5))
        publish(yo, 4, of, N.of, N.c_top)
        publish(yo, 5, of, N.of, N.c_top)
        publish(xo, 5, os, N.os, N.c_top)
        wait(ut45, N.t45)
        wait(xt5.at[pl.ds(0, 15 * 256)], N.tx5)
        keep(xo, 4, own(yo, 4).astype(F32) - dot(ut45[...], xt5[...]), uib)
        for d in range(1, 8):
            send(own_at(xo, 4), rows(xt4, (q % 8) * 256, 256, 256), N.c_top, N.tx4, dev(q ^ d, k, z), 2)
        put(xt4, (q % 8) * 256, 256, own(xo, 4))
        for j in range(8):
            zz = (4 - (q // 8) * 4 + j) % 8

            @when(zz != z)
            def _(zz=zz):
                send_raw(rows(xt5, zz * 512, 512, 512), xb5, N.c_top, N.x5, dev(q, k, zz))

        sent[N.c_top] += 28
        xb5[...] = xt5[pl.ds(pl.multiple_of(z * 512, 512), 512), :]

        @when(not_quad)
        def _():
            wait(ub.at[pl.ds(0, 384)], N.s_ub)
            leaf_one()

        wait(ut35, N.t35)
        acc[...] = own(yo, 3).astype(F32) - dot(ut35[...], xt5[...])
        wait(xt4.at[pl.ds(0, 7 * 256)], N.tx4)

        for j in range(4):
            zz = (q // 8) * 4 + j
            src = rows(xt4, j * 512, 512, 512)

            @when(zz == z)
            def _(src=src):
                local(src, xb4, N.xl)
                wait(xb4, N.xl)

            @when(zz != z)
            def _(src=src, zz=zz):
                send_raw(src, xb4, N.c_x4, N.x4, dev(q, k, zz))

        wait(ut34, N.t34)
        keep(xo, 3, acc[...] - dot(ut34[...], xt4[...]), uib)
        at = rows(xb3, half * 256, 256, 256)
        for d in range(1, 4):
            @when(zd == top)
            def _(d=d):
                send_raw(own_at(xo, 3), at, N.c_top, N.x3, dev(q ^ d, k, z))

            @when(zd != top)
            def _(d=d):
                send_raw(own_at(xo, 3), at, N.c_top, N.x3, dev(q ^ d, k, zd))

        sent[N.c_top] += 6

        @when(zd == top)
        def _():
            put(xb3, half * 256, 256, own(xo, 3))

        @when(zd != top)
        def _():
            send(own_at(xo, 3), at, N.c_top_far, N.x3, dev(q, k, zd), 2)

    @when(jnp.logical_or(not_top, quad))
    def _():
        wait(ub.at[pl.ds(0, 384)], N.s_ub)

    @when(not_top)
    def _():
        wait(xb5, N.x5)

    @when(not_quad)
    def _():
        @when(both(turn == 1, not_top))
        def _():
            leaf_one()
            sent[N.c_leaf1] = 6

        @when(is_leaf)
        def _():
            for w in order:
                add_up(w, 1024, xb5, True)
                onward(w, 2, 0, N.c_leaf)

        @when(turn == 2)
        def _():
            for w in order:
                add_up(w, 1024, xb5, True)
            for w in order:
                take(w, 0)

                @when(high)
                def _(w=w):
                    take(w, 1)

                onward(w, jnp.where(high, 3, 0), 0, N.c_mid)

        @when(is_end)
        def _():
            for w in order:
                add_up(w, 1024, xb5, True)
            for w in order:
                take(w, 0)

                @when(low_end)
                def _(w=w):
                    take(w, 1)

                to_diag(w, 2, N.c_exit)

    @when(quad)
    def _():
        for w in order:
            add_up(w, 1024, xb5, True)

        @when(not_top)
        def _():
            wait(xb4, N.x4)

        @when(pair)
        def _():
            for w in order:
                add_up(w, 512, xb4)
            mine_too = both(is_top, diag)

            @when(mine_too)
            def _():
                wait(xb3.at[pl.ds(0, 256)], N.x3)

            @when(jnp.logical_not(mine_too))
            def _():
                wait(xb3, N.x3)

            for w in order:
                add_up(w, 0, xb3)

                @when(not_diag)
                def _(w=w):
                    to_diag(w, 0, N.c_near)

        @when(not_pair)
        def _():
            close = jnp.logical_or(z % 4 == 1, z % 4 == 2)

            @when(jnp.logical_not(close))
            def _():
                for w in order:
                    add_up(w, 512, xb4)
                    here = pl.ds(w * 256, 256)
                    bpb[here, :] = bpart[here, :].astype(BF)
                    send(bpb.at[here], tb.at[0, here], N.c_sidefar, N.sd0 + w, dev(q, k, z ^ 1), 2)

            @when(close)
            def _():
                for w in order:
                    add_up(w, 512, xb4)
                    here = pl.ds(w * 256, 256)
                    wait(tb.at[0, here], N.sd0 + w)
                    bpart[here, :] += tb[0, here, :].astype(F32)
                    to_diag(w, 1, N.c_side)

    @when(diag)
    def _():
        def rest(w):
            wait(fb.at[w], N.fb0 + w)
            value = own(yo, w).astype(F32) - bpart[pl.ds(w * 256, 256), :]
            for i in range(3):
                value -= fb[w, pl.ds(i * 256, 256), :].astype(F32)
            return value

        keep(xo, 2, rest(2), uib)
        send(own_at(xo, 2), rows(xc2, place, 256, 256), N.c_diag, N.cx2, dev(q ^ 1, k, z), 2)
        put(xc2, place, 256, own(xo, 2))
        publish(xo, 2, os, N.os, N.c_diag)
        r1 = rest(1)
        acc[...] = rest(0)
        wait(yt4.at[pl.ds(0, 1280)], N.s_ud)
        wait(xc2.at[pl.ds(0, 256)], N.cx2)
        keep(xo, 1, r1 - dot(u12[...], xc2[...]), uib)
        publish(xo, 1, os, N.os, N.c_diag)
        keep(xo, 0, acc[...] - dot(u02[...], xc2[...]) - dot(u01[...], own(xo, 1)), uib)
        publish(xo, 0, os, N.os, N.c_diag)

    @when(is_top)
    def _():
        for level in (4, 3):
            publish(xo, level, os, N.os, N.c_top)

    wait(of, N.of)
    wait(os, N.os)

    @when(both(is_top, quad))
    def _():
        wait(yt4.at[pl.ds(0, 12 * 128)], N.c_x4)

    @when(both(is_top, not_quad))
    def _():
        wait(yt4.at[pl.ds(0, 16 * 128)], N.c_x4)

    where = {
        N.c_all: None, N.c_diag: diag, N.c_ntop: not_top, N.c_quad: quad, N.c_quad_ntop: both(quad, not_top),
        N.c_quad_top: both(quad, is_top), N.c_pair_ntop: both(pair, not_top), N.c_top: is_top, N.c_top_far: far, N.c_spread: not_quad,
        N.c_leaf: both(not_quad, is_leaf), N.c_leaf1: both(not_quad, turn == 1), N.c_mid: both(not_quad, turn == 2),
        N.c_exit: both(not_quad, is_end), N.c_near: both(pair, not_diag),
        N.c_side: both(both(quad, not_pair), jnp.logical_or(z % 4 == 1, z % 4 == 2)),
        N.c_sidefar: both(both(quad, not_pair), jnp.logical_or(z % 4 == 0, z % 4 == 3)),
        N.c_pair: pair, N.c_npair: not_pair, N.c_npair2: not_pair,
    }
    del sent[N.c_u45]
    for cond, units in sent.items():
        def drain(cond=cond, units=units):
            left = int(units * 128)
            while left > 0:
                now = min(left, 4096)
                wait(yt4.at[pl.ds(0, now)], cond)
                left -= now

        if where[cond] is None:
            drain()
        else:
            when(where[cond])(drain)


def on_device(right_side, l_factor, u_factor, l_pattern, u_pattern, l_inverse, u_inverse):
    vm = lambda *shape: pltpu.VMEM(shape, BF)
    anywhere = pl.BlockSpec(memory_space=pl.ANY)
    scratch = [
        pltpu.SMEM((6, 24), jnp.int32), pltpu.SMEM((6, 24), jnp.int32),
        vm(2, 768, 128), vm(2, 6, 128, 128), vm(2, 6, 128, 128),
        vm(640, 3072), vm(640, 3072),
        vm(256, 256), vm(256, 1024), vm(768, 2048), vm(768, 1536), vm(256, 512), vm(256, 512), vm(256, 256),
        vm(256, 512), vm(384, 512),
        vm(256, 2048), vm(256, 4096), vm(256, 4096), vm(256, 2048), vm(256, 4096),
        vm(1536, 128), vm(1536, 128), vm(1536, 128), vm(768, 128),
        vm(512, 128), vm(1024, 128), vm(2048, 128),
        vm(4096, 128), vm(4096, 128), vm(4096, 128), vm(2048, 128),
        vm(512, 128), vm(512, 128), vm(512, 128), vm(512, 128),
        pltpu.VMEM((256, 128), F32), pltpu.VMEM((768, 128), F32), vm(768, 128),
        vm(3, 768, 128), vm(2, 768, 128), vm(512, 128),
        pltpu.SemaphoreType.DMA((85,)),
    ]
    return pl.pallas_call(
        kernel,
        out_shape=(jax.ShapeDtypeStruct((768, 256), BF), jax.ShapeDtypeStruct((768, 256), BF)),
        in_specs=[anywhere] * 7,
        out_specs=(anywhere, anywhere),
        scratch_shapes=scratch,
        compiler_params=pltpu.CompilerParams(collective_id=0, has_side_effects=True, vmem_limit_bytes=VMEM_LIMIT),
        name="sweeps",
    )(right_side, l_factor, u_factor, l_pattern, u_pattern, l_inverse, u_inverse)


def solution(mesh):
    placed = (
        P("prow", None),
        P("prow", "pcol"),
        P("prow", "pcol"),
        P("prow", "pcol"),
        P("prow", "pcol"),
        P("prow", None, None),
        P("prow", None, None),
    )
    return jax.shard_map(
        on_device,
        mesh=mesh,
        in_specs=placed,
        out_specs=(P("prow", None), P("prow", None)),
        check_vma=False,
    )
```

```python
import jax
import jax.numpy as jnp
from jax import lax
from jax.experimental import pallas as pl
from jax.experimental.pallas import tpu as pltpu
from jax.sharding import PartitionSpec as P

MESH = pl.DeviceIdType.MESH
BF = jnp.bfloat16
F32 = jnp.float32
VMEM_LIMIT = 62 * 2**20

class N:
    (
        rhs, li, ui, lp, up, l1, l2, l3, l4, l5, u0, u1, u2, u3, u4, s_rhs, s_li, s_ui, s_l1, s_l2, s_lb, s_ub, s_ud,
        y0, y1, y2, sc, ag, sc2, ag2, y3, f3, f4, f5, t43, t54, t45, t34, t35, ty3a, ty3b, ty4, tx5, tx4, x5, x4, x3,
        sd0, sd1, sd2, tr10, tr11, tr12, tr20, tr21, tr22, fb0, fb1, fb2, cx2, of, os, xl, c_all, c_diag, c_ntop,
        c_quad, c_quad_ntop, c_quad_top, c_pair_ntop, c_top, c_top_far, c_x4, c_spread, c_pair, c_npair, c_npair2,
        c_u45, c_sidefar, c_leaf, c_leaf1, c_mid, c_exit, c_near, c_side,
    ) = range(85)


def dot(a, b):
    return jnp.dot(a, b, preferred_element_type=F32)


def kernel(
    rhs, lf, uf, lph, uph, li, ui, of, os,
    lp, up, rb, lib, uib, ls, us, l1b, l2b, lb, ub, u12, u02, u01,
    mtl, mtu, lt43, lt54, ut45, ut34, ut35,
    yo, xo, yb, part, f3, f4, f5, yt3, yt4, xt5, xt4, xb5, xb4, xb3, yb3, acc, bpart, bpb, fb, tb, xc2,
    sem,
):
    p = lax.axis_index("prow")
    z = lax.axis_index("pcol")
    q, k = p // 2, p % 2
    zd = q // 2
    half = q % 2
    top = 1 + 4 * k
    other_top = 5 - 4 * k
    block_row = z // 2
    diag = z == zd
    pair = block_row == q // 4
    quad = z // 4 == q // 8
    is_top = z == top
    not_top = z != top
    not_diag = z != zd
    not_pair = block_row != q // 4
    not_quad = z // 4 != q // 8
    me = pl.multiple_of(k * 128, 128)
    both = jnp.logical_and

    def S(name):
        return sem.at[name]

    def dev(qq, kk, zz):
        return (qq * 2 + kk, zz)

    sent = {}

    def send_raw(src, dst, cond, rsem, device):
        pltpu.make_async_remote_copy(
            src_ref=src, dst_ref=dst, send_sem=S(cond), recv_sem=S(rsem), device_id=device, device_id_type=MESH
        ).start()

    def send(src, dst, cond, rsem, device, units):
        send_raw(src, dst, cond, rsem, device)
        sent[cond] = sent.get(cond, 0) + units

    def local(src, dst, s):
        pltpu.make_async_copy(src, dst, S(s)).start()

    def wait(ref, s):
        pltpu.make_async_copy(ref, ref, S(s)).wait()

    def rows(ref, start, size, align=128):
        return ref.at[pl.ds(pl.multiple_of(start, align), size)]

    when = pl.when
    sib = dev(q, 1 - k, z)

    bar = pltpu.get_barrier_semaphore()

    def hello(device):
        pl.semaphore_signal(bar, inc=1, device_id=device, device_id_type=MESH)

    for d in range(1, 16):
        hello(dev(q ^ d, k, z))
    for j in range(1, 8):
        hello(dev(q, k, (z + j) % 8))
    for j in range(8):
        hello(dev(q, 1 - k, (z + j) % 8))
    far = both(is_top, zd != top)
    near = both(not_top, pair)
    near_diag = both(near, diag)
    near_rest = both(near, not_diag)

    @when(far)
    def _():
        for d in range(1, 4):
            hello(dev(q ^ d, k, zd))

    @when(near_diag)
    def _():
        hello(dev(q ^ 1, k, top))

    @when(near_rest)
    def _():
        hello(dev(2 * z, k, top))
        hello(dev(2 * z + 1, k, top))

    local(rhs.at[:, pl.ds(me, 128)], rb.at[k], N.rhs)
    local(li, lib.at[k], N.li)
    local(lph, lp, N.lp)
    local(uph, up, N.up)

    @when(diag)
    def _():
        for v in (1, 2):
            local(lf.at[pl.ds(v * 128, 128), :], ls.at[pl.ds((v - 1) * 128, 128), :], N.l1 + v - 1)

    for v in (4, 5, 3):
        local(lf.at[pl.ds(v * 128, 128), :], ls.at[pl.ds((v - 1) * 128, 128), :], N.l1 + v - 1)
    local(ui, uib.at[k], N.ui)
    for w in (4, 3, 0, 1, 2):
        local(uf.at[pl.ds(w * 128, 128), :], us.at[pl.ds(w * 128, 128), :], N.u0 + w)

    def mask(stage, pattern, srow, prow, col, dst, drow, dcol):
        block = stage[pl.ds(srow, 128), pl.ds(pl.multiple_of(col * 128, 128), 128)]
        keep = jnp.full((128, 128), pattern[prow, col].astype(F32)).astype(BF)
        dst[pl.ds(pl.multiple_of(drow, 128), 128), pl.ds(pl.multiple_of(dcol, 128), 128)] = block * keep

    def each_group(body):
        def step(j, carry):
            body(j)
            return carry

        lax.fori_loop(0, 4, step, 0)

    def each_own(body):
        for j2 in range(2):
            body(j2, 2 * half + j2)

    pltpu.make_async_copy(lph, lp, S(N.lp)).wait()
    pltpu.make_async_copy(uph, up, S(N.up)).wait()

    @when(diag)
    def _():
        wait(ls.at[pl.ds(0, 128), :], N.l1)
        each_own(lambda j2, j: mask(ls, lp, 0, 1, j * 6, l1b, me, j2 * 128))
        wait(ls.at[pl.ds(128, 128), :], N.l2)

        def level2(j):
            for w in range(2):
                mask(ls, lp, 128, 2, j * 6 + w, l2b, me, w * 512 + j * 128)

        each_group(level2)

    wait(ls.at[pl.ds(384, 128), :], N.l4)
    wait(ls.at[pl.ds(512, 128), :], N.l5)

    def lower_top(j):
        mask(ls, lp, 384, 4, j * 6 + 3, mtl, 0, j * 128)
        mask(ls, lp, 512, 5, j * 6 + 4, mtl, 128, j * 128)

    each_group(lower_top)

    for cond, count in ((far, 33), (near_diag, 31), (near_rest, 32)):
        @when(cond)
        def _(count=count):
            pl.semaphore_wait(bar, count)

    @when(jnp.logical_not(jnp.logical_or(far, near)))
    def _():
        pl.semaphore_wait(bar, 30)

    send(rhs.at[:, pl.ds(pl.multiple_of((1 - k) * 128, 128), 128)], rb.at[k], N.c_all, N.s_rhs, sib, 6)
    send(li, lib.at[k], N.c_all, N.s_li, sib, 6)

    @when(diag)
    def _():
        send(l1b.at[pl.ds(me, 128)], l1b.at[pl.ds(me, 128)], N.c_diag, N.s_l1, sib, 2)
        send(l2b.at[pl.ds(me, 128)], l2b.at[pl.ds(me, 128)], N.c_diag, N.s_l2, sib, 8)

    def to_top(src, dst, column, name, everywhere, tag=None):
        view = dst.at[pl.ds(me, 128), pl.ds(pl.multiple_of(column * 512, 512), 512)]

        def from_rest():
            cond = tag or (N.c_ntop if everywhere else N.c_quad_ntop)
            send(src, view, cond, name, dev(q, k, top), 4)
            send(src, view, cond, name, dev(q, 1 - k, other_top), 4)

        def from_top():
            local(src, view, name)
            send(src, view, N.c_top if everywhere else N.c_quad_top, name, dev(q, 1 - k, other_top), 4)

        for mine, go in ((not_top, from_rest), (is_top, from_top)):
            when(mine if everywhere else both(mine, quad))(go)

    to_top(mtl.at[pl.ds(0, 128)], lt43, z % 4, N.t43, False)
    to_top(mtl.at[pl.ds(128, 128)], lt54, z, N.t54, True)

    def solve(inverse, level, resid):
        for g in range(2):
            piece = resid[g * 128 : (g + 1) * 128].astype(BF)
            yield dot(inverse[g, level], piece).astype(BF)

    def right(level):
        return jnp.concatenate([rb[g, pl.ds(level * 128, 128), :] for g in range(2)], axis=0).astype(F32)

    def keep(store, level, resid, inverse):
        for g, value in enumerate(solve(inverse, level, resid)):
            store[pl.ds(level * 256 + g * 128, 128), :] = value

    def own(store, level):
        return store[pl.ds(level * 256, 256), :]

    def own_at(store, level):
        return store.at[pl.ds(level * 256, 256)]

    def put(ref, start, size, value):
        ref[pl.ds(pl.multiple_of(start, size), size), :] = value

    wait(rb.at[0], N.rhs)
    wait(lib.at[0], N.li)
    wait(rb.at[0], N.s_rhs)
    wait(lib.at[0], N.s_li)
    keep(yo, 0, right(0), lib)
    place = half * 256

    def spread(level):
        for d in range(1, 4 if level < 2 else 8):
            send(own_at(yo, level), rows(yb, level * 512 + place, 256), N.c_diag, N.y0 + level, dev(q ^ d, k, z), 2)

    @when(diag)
    def _():
        spread(0)
        wait(l1b.at[pl.ds(0, 128)], N.s_l1)
        keep(yo, 1, right(1) - dot(l1b[...], own(yo, 0)), lib)
        spread(1)
        put(yb, place, 256, own(yo, 0))
        put(yb, 512 + place, 256, own(yo, 1))

    wait(ls.at[pl.ds(256, 128), :], N.l3)
    for v in (3, 4, 5):
        def low(j, v=v):
            for w in range(3 if v < 5 else 4):
                mask(ls, lp, (v - 1) * 128, v, j * 6 + w, lb, (v - 3) * 256 + me, w * 512 + j * 128)

        each_group(low)
        width = 1536 if v < 5 else 2048
        mine = lb.at[pl.ds(pl.multiple_of((v - 3) * 256 + me, 128), 128), pl.ds(0, width)]
        send(mine, mine, N.c_all, N.s_lb, sib, width // 128)

    @when(diag)
    def _():
        wait(l2b.at[pl.ds(0, 128)], N.s_l2)
        wait(yb.at[pl.ds(0, 256)], N.y0)
        wait(yb.at[pl.ds(0, 256)], N.y1)
        keep(yo, 2, right(2) - dot(l2b[...], yb[pl.ds(0, 1024), :]), lib)
        spread(2)
        put(yb, 1024 + place, 256, own(yo, 2))

    wait(us.at[pl.ds(512, 128), :], N.u4)
    each_group(lambda j: mask(us, up, 512, 4, j * 6 + 5, mtu, 0, j * 128))
    wait(us.at[pl.ds(384, 128), :], N.u3)

    def upper3(j):
        mask(us, up, 384, 3, j * 6 + 4, mtu, 128, j * 128)
        mask(us, up, 384, 3, j * 6 + 5, mtu, 256, j * 128)

    each_group(upper3)
    wait(uib.at[0], N.ui)
    send(uib.at[k], uib.at[k], N.c_all, N.s_ui, sib, 6)
    def fold_at(level):
        return pl.ds((level - 3) * 256, 256)

    def fold_here(level, dst, slot):
        put(dst, slot * 256, 256, part[fold_at(level), :])

    def fold_there(level, dst, slot, cond, name):
        send(part.at[fold_at(level)], rows(dst, slot * 256, 256), cond, name, dev(q, k, top), 2)

    def low_part(level):
        return dot(lb[fold_at(level), pl.ds(0, 1536)], yb[...])

    wait(lb.at[pl.ds(0, 320)], N.s_lb)

    def piece(owner):
        return rows(yb, owner * 64, 64, 64)

    @when(both(pair, not_diag))
    def _():
        wait(yb.at[pl.ds(0, 512)], N.y0)
        wait(yb.at[pl.ds(0, 512)], N.y1)

    @when(pair)
    def _():
        for d in (4, 8, 12):
            send(piece(q ^ d), piece(q ^ d), N.c_pair, N.sc, dev(q ^ d, k, z), 1 / 2)
        for d in range(4, 16):
            send(piece(q), piece(q), N.c_pair, N.ag, dev(q ^ d, k, z), 1 / 2)

    @when(not_pair)
    def _():
        wait(yb.at[pl.ds(0, 64)], N.sc)
        for d in range(1, 4):
            send(piece(q), piece(q), N.c_npair, N.ag, dev(q ^ d, k, z), 1 / 2)
        for e in range(1, 4):
            @when((q // 4) ^ e != block_row)
            def _(e=e):
                for d in range(4 * e, 4 * e + 4):
                    send_raw(piece(q), piece(q), N.c_npair2, N.ag, dev(q ^ d, k, z))

    sent[N.c_npair2] = 4
    for w in range(3):
        wait(us.at[pl.ds(w * 128, 128), :], N.u0 + w)

        def high(j, w=w):
            for v in (3, 4, 5):
                mask(us, up, w * 128, w, j * 6 + v, ub, w * 256 + me, (v - 3) * 512 + j * 128)

        each_group(high)
        mine = rows(ub, w * 256 + me, 128)
        send(mine, mine, N.c_all, N.s_ub, sib, 12)

    @when(diag)
    def _():
        def near_columns(j):
            mask(us, up, 128, 1, j * 6 + 2, u12, me, j * 128)
            mask(us, up, 0, 0, j * 6 + 2, u02, me, j * 128)

        each_group(near_columns)
        each_own(lambda j2, j: mask(us, up, 0, 0, j * 6 + 1, u01, me, j2 * 128))
        for ref, units in ((u12, 4), (u02, 4), (u01, 2)):
            send(ref.at[pl.ds(me, 128)], ref.at[pl.ds(me, 128)], N.c_diag, N.s_ud, sib, units)

    @when(diag)
    def _():
        wait(yb.at[pl.ds(0, 256)], N.y2)

    @when(both(quad, not_diag))
    def _():
        wait(yb.at[pl.ds(0, 512)], N.y2)

    @when(not_pair)
    def _():
        wait(yb.at[pl.ds(0, 15 * 64)], N.ag)

    def fold(level, dst, slot, cond, name):
        part[fold_at(level), :] = low_part(level).astype(BF)

        @when(is_top)
        def _():
            fold_here(level, dst, slot)

        @when(not_top)
        def _():
            fold_there(level, dst, slot, cond, name)

    @when(pair)
    def _():
        fold(3, f3, z % 2, N.c_pair_ntop, N.f3)

    eighth = rows(yb, 1024 + (q % 8) * 64, 64, 64)

    @when(quad)
    def _():
        fold(4, f4, z % 4, N.c_quad_ntop, N.f4)
        send(eighth, eighth, N.c_quad, N.sc2, dev(q ^ 8, k, z), 1 / 2)

    def total(ref, count):
        value = ref[pl.ds(0, 256), :].astype(F32)
        for i in range(1, count):
            value += ref[pl.ds(i * 256, 256), :].astype(F32)
        return value

    @when(is_top)
    def _():
        @when(pair)
        def _():
            wait(f3.at[pl.ds(0, 256)], N.f3)

        @when(not_pair)
        def _():
            wait(f3, N.f3)

        keep(yo, 3, right(3) - total(f3, 2), lib)
        for d in range(1, 8):
            send(own_at(yo, 3), rows(yt3, q * 256, 256, 256), N.c_top, N.ty3a, dev(q ^ d, k, z), 2)
        for d in range(8, 16):
            send(own_at(yo, 3), rows(yt3, q * 256, 256, 256), N.c_top, N.ty3b, dev(q ^ d, k, z), 2)
        put(yt3, q * 256, 256, own(yo, 3))

    @when(not_quad)
    def _():
        wait(yb.at[pl.ds(0, 64)], N.sc2)
        for d in range(1, 8):
            send(eighth, eighth, N.c_spread, N.ag2, dev(q ^ d, k, z), 1 / 2)
        wait(yb.at[pl.ds(0, 7 * 64)], N.ag2)

    acc[...] = low_part(5)

    to_top(mtu.at[pl.ds(0, 128)], ut45, z, N.t45, True, N.c_u45)
    to_top(mtu.at[pl.ds(128, 128)], ut34, z % 4, N.t34, False)

    def sum5():
        mixed = acc[...] + dot(lb[fold_at(5), pl.ds(1536, 512)], yb3[...])
        part[fold_at(5), :] = mixed.astype(BF)

    @when(not_top)
    def _():
        wait(yb3, N.y3)
        sum5()
        fold_there(5, f5, z, N.c_ntop, N.f5)

    def publish(store, level, out, name, cond):
        dst = out.at[pl.ds(level * 128, 128), pl.ds(me, 128)]
        for j, flip in [(j, flip) for j in (4, 3, 5, 2, 6, 1, 7, 0) for flip in (0, 1)]:
                core = (k + flip) % 2
                src = rows(store, level * 256 + core * 128, 128)
                if flip == 0 and j == 0:
                    local(src, dst, name)
                else:
                    send(src, dst, cond, name, dev(q, core, (z + j) % 8), 1)

    out0 = of.at[pl.ds(0, 128), pl.ds(me, 128)]
    local(rows(yo, me, 128), out0, N.of)
    send(rows(yo, pl.multiple_of((1 - k) * 128, 128), 128), out0, N.c_all, N.of, sib, 1)
    wait(uib.at[0], N.s_ui)

    @when(not_top)
    def _():
        wait(yt4.at[pl.ds(0, 8 * 128)], N.c_u45)

    to_top(mtu.at[pl.ds(256, 128)], ut35, z, N.t35, True)

    @when(diag)
    def _():
        publish(yo, 1, of, N.of, N.c_diag)
        publish(yo, 2, of, N.of, N.c_diag)

    order = (2, 1, 0)

    def add_up(w, columns, x, first=False):
        here = pl.ds(w * 256, 256)
        value = dot(ub[here, pl.ds(columns, 512)], x[...])
        bpart[here, :] = value if first else bpart[here, :] + value

    def to_diag(w, slot, cond):
        here = pl.ds(w * 256, 256)
        bpb[here, :] = bpart[here, :].astype(BF)
        send(bpb.at[here], fb.at[w, pl.ds(pl.multiple_of(slot * 256, 256), 256)], cond, N.fb0 + w, dev(q, k, zd), 2)

    high = zd % 4 < 2
    low_end = zd % 4 >= 2
    turn = z % 4
    base = (z // 4) * 4

    def onward(w, target, slot, cond):
        here = pl.ds(w * 256, 256)
        bpb[here, :] = bpart[here, :].astype(BF)
        send(bpb.at[here], tb.at[slot, here], cond, ((N.tr10, N.tr11, N.tr12), (N.tr20, N.tr21, N.tr22))[slot][w], dev(q, k, base + target), 2)

    def take(w, slot):
        here = pl.ds(w * 256, 256)
        wait(tb.at[slot, here], ((N.tr10, N.tr11, N.tr12), (N.tr20, N.tr21, N.tr22))[slot][w])
        bpart[here, :] += tb[slot, here, :].astype(F32)

    def leaf_one():
        for w in order:
            add_up(w, 1024, xb5, True)
            onward(w, jnp.where(high, 2, 0), 1, N.c_leaf1)

    is_end = turn == jnp.where(high, 3, 0)
    is_leaf = turn == jnp.where(high, 0, 3)

    @when(is_top)
    def _():
        wait(yt3.at[pl.ds(0, 7 * 256)], N.ty3a)
        wait(yt3.at[pl.ds(0, 8 * 256)], N.ty3b)
        for j in range(1, 8):
            zz = (z + j) % 8
            send(rows(yt3, zz * 512, 512, 512), yb3, N.c_top, N.y3, dev(q, k, zz), 4)
        yb3[...] = yt3[pl.ds(pl.multiple_of(z * 512, 512), 512), :]

        @when(quad)
        def _():
            wait(f4.at[pl.ds(0, 768)], N.f4)

        @when(not_quad)
        def _():
            wait(f4, N.f4)

        s4 = right(4) - total(f4, 4)
        wait(lt43, N.t43)
        eight = pl.ds(pl.multiple_of((q // 8) * 2048, 2048), 2048)
        keep(yo, 4, s4 - dot(lt43[...], yt3[eight, :]), lib)
        for d in range(1, 16):
            send(own_at(yo, 4), rows(yt4, q * 256, 256, 256), N.c_top, N.ty4, dev(q ^ d, k, z), 2)
        put(yt4, q * 256, 256, own(yo, 4))
        sum5()
        fold_here(5, f5, z)
        publish(yo, 3, of, N.of, N.c_top)
        wait(f5.at[pl.ds(0, 7 * 256)], N.f5)
        acc[...] = right(5) - total(f5, 8)
        wait(lt54, N.t54)
        wait(yt4.at[pl.ds(0, 15 * 256)], N.ty4)
        keep(yo, 5, acc[...] - dot(lt54[...], yt4[...]), lib)
        keep(xo, 5, own(yo, 5).astype(F32), uib)
        for d in range(1, 16):
            send(own_at(xo, 5), rows(xt5, q * 256, 256, 256), N.c_top, N.tx5, dev(q ^ d, k, z), 2)
        put(xt5, q * 256, 256, own(xo, 5))
        publish(yo, 4, of, N.of, N.c_top)
        publish(yo, 5, of, N.of, N.c_top)
        publish(xo, 5, os, N.os, N.c_top)
        wait(xt5.at[pl.ds(0, 15 * 256)], N.tx5)
        for j in range(8):
            zz = (4 - (q // 8) * 4 + j) % 8

            @when(zz != z)
            def _(zz=zz):
                send_raw(rows(xt5, zz * 512, 512, 512), xb5, N.c_top, N.x5, dev(q, k, zz))

        sent[N.c_top] += 28
        xb5[...] = xt5[pl.ds(pl.multiple_of(z * 512, 512), 512), :]
        wait(ut45, N.t45)
        keep(xo, 4, own(yo, 4).astype(F32) - dot(ut45[...], xt5[...]), uib)
        for d in range(1, 8):
            send(own_at(xo, 4), rows(xt4, (q % 8) * 256, 256, 256), N.c_top, N.tx4, dev(q ^ d, k, z), 2)
        put(xt4, (q % 8) * 256, 256, own(xo, 4))

        @when(not_quad)
        def _():
            wait(ub.at[pl.ds(0, 384)], N.s_ub)
            leaf_one()

        wait(ut35, N.t35)
        acc[...] = own(yo, 3).astype(F32) - dot(ut35[...], xt5[...])
        wait(xt4.at[pl.ds(0, 7 * 256)], N.tx4)

        for j in range(4):
            zz = (q // 8) * 4 + j
            src = rows(xt4, j * 512, 512, 512)

            @when(zz == z)
            def _(src=src):
                local(src, xb4, N.xl)
                wait(xb4, N.xl)

            @when(zz != z)
            def _(src=src, zz=zz):
                send_raw(src, xb4, N.c_x4, N.x4, dev(q, k, zz))

        wait(ut34, N.t34)
        keep(xo, 3, acc[...] - dot(ut34[...], xt4[...]), uib)
        at = rows(xb3, half * 256, 256, 256)
        for d in range(1, 4):
            @when(zd == top)
            def _(d=d):
                send_raw(own_at(xo, 3), at, N.c_top, N.x3, dev(q ^ d, k, z))

            @when(zd != top)
            def _(d=d):
                send_raw(own_at(xo, 3), at, N.c_top, N.x3, dev(q ^ d, k, zd))

        sent[N.c_top] += 6

        @when(zd == top)
        def _():
            put(xb3, half * 256, 256, own(xo, 3))

        @when(zd != top)
        def _():
            send(own_at(xo, 3), at, N.c_top_far, N.x3, dev(q, k, zd), 2)

    @when(jnp.logical_or(not_top, quad))
    def _():
        wait(ub.at[pl.ds(0, 384)], N.s_ub)

    @when(not_top)
    def _():
        wait(xb5, N.x5)

    @when(not_quad)
    def _():
        @when(both(turn == 1, not_top))
        def _():
            leaf_one()
            sent[N.c_leaf1] = 6

        @when(is_leaf)
        def _():
            for w in order:
                add_up(w, 1024, xb5, True)
                onward(w, 2, 0, N.c_leaf)

        @when(turn == 2)
        def _():
            for w in order:
                add_up(w, 1024, xb5, True)
            for w in order:
                take(w, 0)

                @when(high)
                def _(w=w):
                    take(w, 1)

                onward(w, jnp.where(high, 3, 0), 0, N.c_mid)

        @when(is_end)
        def _():
            for w in order:
                add_up(w, 1024, xb5, True)
            for w in order:
                take(w, 0)

                @when(low_end)
                def _(w=w):
                    take(w, 1)

                to_diag(w, 2, N.c_exit)

    @when(quad)
    def _():
        for w in order:
            add_up(w, 1024, xb5, True)

        @when(not_top)
        def _():
            wait(xb4, N.x4)

        @when(pair)
        def _():
            for w in order:
                add_up(w, 512, xb4)
            mine_too = both(is_top, diag)

            @when(mine_too)
            def _():
                wait(xb3.at[pl.ds(0, 256)], N.x3)

            @when(jnp.logical_not(mine_too))
            def _():
                wait(xb3, N.x3)

            for w in order:
                add_up(w, 0, xb3)

                @when(not_diag)
                def _(w=w):
                    to_diag(w, 0, N.c_near)

        @when(not_pair)
        def _():
            close = jnp.logical_or(z % 4 == 1, z % 4 == 2)

            @when(jnp.logical_not(close))
            def _():
                for w in order:
                    add_up(w, 512, xb4)
                    here = pl.ds(w * 256, 256)
                    bpb[here, :] = bpart[here, :].astype(BF)
                    send(bpb.at[here], tb.at[0, here], N.c_sidefar, N.sd0 + w, dev(q, k, z ^ 1), 2)

            @when(close)
            def _():
                for w in order:
                    add_up(w, 512, xb4)
                    here = pl.ds(w * 256, 256)
                    wait(tb.at[0, here], N.sd0 + w)
                    bpart[here, :] += tb[0, here, :].astype(F32)
                    to_diag(w, 1, N.c_side)

    @when(diag)
    def _():
        def rest(w):
            wait(fb.at[w], N.fb0 + w)
            value = own(yo, w).astype(F32) - bpart[pl.ds(w * 256, 256), :]
            for i in range(3):
                value -= fb[w, pl.ds(i * 256, 256), :].astype(F32)
            return value

        keep(xo, 2, rest(2), uib)
        send(own_at(xo, 2), rows(xc2, place, 256, 256), N.c_diag, N.cx2, dev(q ^ 1, k, z), 2)
        put(xc2, place, 256, own(xo, 2))
        publish(xo, 2, os, N.os, N.c_diag)
        r1 = rest(1)
        acc[...] = rest(0)
        wait(yt4.at[pl.ds(0, 1280)], N.s_ud)
        wait(xc2.at[pl.ds(0, 256)], N.cx2)
        keep(xo, 1, r1 - dot(u12[...], xc2[...]), uib)
        publish(xo, 1, os, N.os, N.c_diag)
        keep(xo, 0, acc[...] - dot(u02[...], xc2[...]) - dot(u01[...], own(xo, 1)), uib)
        publish(xo, 0, os, N.os, N.c_diag)

    @when(is_top)
    def _():
        for level in (4, 3):
            publish(xo, level, os, N.os, N.c_top)

    wait(of, N.of)
    wait(os, N.os)

    @when(both(is_top, quad))
    def _():
        wait(yt4.at[pl.ds(0, 12 * 128)], N.c_x4)

    @when(both(is_top, not_quad))
    def _():
        wait(yt4.at[pl.ds(0, 16 * 128)], N.c_x4)

    where = {
        N.c_all: None, N.c_diag: diag, N.c_ntop: not_top, N.c_quad: quad, N.c_quad_ntop: both(quad, not_top),
        N.c_quad_top: both(quad, is_top), N.c_pair_ntop: both(pair, not_top), N.c_top: is_top, N.c_top_far: far, N.c_spread: not_quad,
        N.c_leaf: both(not_quad, is_leaf), N.c_leaf1: both(not_quad, turn == 1), N.c_mid: both(not_quad, turn == 2),
        N.c_exit: both(not_quad, is_end), N.c_near: both(pair, not_diag),
        N.c_side: both(both(quad, not_pair), jnp.logical_or(z % 4 == 1, z % 4 == 2)),
        N.c_sidefar: both(both(quad, not_pair), jnp.logical_or(z % 4 == 0, z % 4 == 3)),
        N.c_pair: pair, N.c_npair: not_pair, N.c_npair2: not_pair,
    }
    del sent[N.c_u45]
    for cond, units in sent.items():
        def drain(cond=cond, units=units):
            left = int(units * 128)
            while left > 0:
                now = min(left, 4096)
                wait(yt4.at[pl.ds(0, now)], cond)
                left -= now

        if where[cond] is None:
            drain()
        else:
            when(where[cond])(drain)


def on_device(right_side, l_factor, u_factor, l_pattern, u_pattern, l_inverse, u_inverse):
    vm = lambda *shape: pltpu.VMEM(shape, BF)
    anywhere = pl.BlockSpec(memory_space=pl.ANY)
    scratch = [
        pltpu.SMEM((6, 24), jnp.int32), pltpu.SMEM((6, 24), jnp.int32),
        vm(2, 768, 128), vm(2, 6, 128, 128), vm(2, 6, 128, 128),
        vm(640, 3072), vm(640, 3072),
        vm(256, 256), vm(256, 1024), vm(768, 2048), vm(768, 1536), vm(256, 512), vm(256, 512), vm(256, 256),
        vm(256, 512), vm(384, 512),
        vm(256, 2048), vm(256, 4096), vm(256, 4096), vm(256, 2048), vm(256, 4096),
        vm(1536, 128), vm(1536, 128), vm(1536, 128), vm(768, 128),
        vm(512, 128), vm(1024, 128), vm(2048, 128),
        vm(4096, 128), vm(4096, 128), vm(4096, 128), vm(2048, 128),
        vm(512, 128), vm(512, 128), vm(512, 128), vm(512, 128),
        pltpu.VMEM((256, 128), F32), pltpu.VMEM((768, 128), F32), vm(768, 128),
        vm(3, 768, 128), vm(2, 768, 128), vm(512, 128),
        pltpu.SemaphoreType.DMA((85,)),
    ]
    return pl.pallas_call(
        kernel,
        out_shape=(jax.ShapeDtypeStruct((768, 256), BF), jax.ShapeDtypeStruct((768, 256), BF)),
        in_specs=[anywhere] * 7,
        out_specs=(anywhere, anywhere),
        scratch_shapes=scratch,
        compiler_params=pltpu.CompilerParams(collective_id=0, has_side_effects=True, vmem_limit_bytes=VMEM_LIMIT),
        name="sweeps",
    )(right_side, l_factor, u_factor, l_pattern, u_pattern, l_inverse, u_inverse)


def solution(mesh):
    placed = (
        P("prow", None),
        P("prow", "pcol"),
        P("prow", "pcol"),
        P("prow", "pcol"),
        P("prow", "pcol"),
        P("prow", None, None),
        P("prow", None, None),
    )
    return jax.shard_map(
        on_device,
        mesh=mesh,
        in_specs=placed,
        out_specs=(P("prow", None), P("prow", None)),
        check_vma=False,
    )
```
